32 devices in a mesh: sect: 2 (over core), cols: 16 (over z, y, x).
Axes of the slice: x: 2, y: 2, z: 4, core: 2. Of those that a mesh axis runs over, the one named last changes fastest.
Arguments:
- air_state: float32 [64, 6, 98304], P('sect', None, 'cols'), may hold values from -6 to 6
- mix_coef: float32 [64, 98304], P('sect', 'cols'), may hold values from 0.1 to 1600
- flux_scale: float32 [98304], P('cols'), may hold values from 0.5 to 4
- sea_state: float32 [6, 98304], P(None, ('sect', 'cols')), may hold values from -6 to 6
- sea_rate: float32 [98304], P(('sect', 'cols')), may hold values from 0.5 to 4
- block_counts: int32 [32, 48], P(('sect', 'cols')), may hold values from 1 to 256, 9830 in all within a row
- cell_column: int32 [393216], P(('sect', 'cols')), may hold values from 0 to 127
- cell_owner: int32 [393216, 1], P(('sect', 'cols')), may hold values from 0 to 31; in each aligned block of 12288 rows (0 to 12287, 12288 to 24575, ...) at most 480 rows name the same one
- cell_coef: float32 [393216], P(('sect', 'cols')), may hold values from 0.3 to 3
- cell_weight: float32 [393216], P(('sect', 'cols')), may hold values from 0.1 to 0.5
- slot_cell: int32 [491520], P(('sect', 'cols')), may hold values from 0 to 3071
- slot_frac: float32 [491520], P(('sect', 'cols')), may hold values from 0.2 to 1
Outputs:
- air_new: float32 [64, 6, 98304], P('sect', None, 'cols')
- sea_new: float32 [6, 98304], P(None, ('sect', 'cols'))
The draws below stay inside these ranges and needn't reach their ends.
Inputs may be any that keep to these rules, and one draw needn't show every extreme that they name: `cell_owner`: among the slots of one device (aligned blocks of 12288 rows) no surface device is named more than 480 times, and some surface device exactly 480 times. `block_counts`: each device's counts have the same sum, and one block of every device is full.
All inputs are finite; a program needn't handle non-finite values.
Results may differ from the reference program's by a relative error of at most 0.0003.
Values sent between devices are 32-bit elements; how exact they have to be, the bound alone decides.
A program may use at most 128 MiB of HBM per device.

```python
import math
import jax
import jax.numpy as jnp
import numpy as np
from jax import lax

TRACERS = 6
LEVELS = 64
BLOCK_COLS = 128
BLOCK_SLOTS = 256
SUBSTEPS = 2
COL_DEV = 6144
COLS = 98304
BLOCKS_DEV = 48
XC_DEV = 12288
XCELLS = 393216
CAP = 480
RECV = 15360
RSLOTS = 491520
SC_DEV = 3072
SURF = 98304
N_SECT = 2
N_COLS = 16


def draw_mix_coef(key, part):
    key_base = jax.random.fold_in(key, 11)
    key_pick = jax.random.fold_in(key, 12)
    key_strength = jax.random.fold_in(key, 13)
    key_forced = jax.random.fold_in(key, 14)
    base = jnp.exp(jax.random.uniform(key_base, (LEVELS, COLS), jnp.float32, math.log(0.1), math.log(4.0)))
    block_total = COLS // BLOCK_COLS
    chosen = jax.random.randint(key_pick, (block_total,), 0, 4) == 0
    forced = jnp.arange(block_total, dtype=jnp.int32) == jax.random.randint(key_forced, (), 0, block_total)
    chosen = jnp.logical_or(chosen, forced)
    strength = jnp.exp(jax.random.uniform(key_strength, (block_total,), jnp.float32, math.log(100.0), math.log(400.0)))
    factor = jnp.where(chosen, strength, jnp.float32(1.0))
    factor_cols = jnp.repeat(factor, BLOCK_COLS, total_repeat_length=COLS)
    level = jnp.arange(LEVELS, dtype=jnp.int32)[:, None]
    boosted = jnp.where(level < LEVELS - 1, base * factor_cols[None, :], base)
    return boosted.astype(jnp.float32)


def touch_ends(values, rng, least, high):
    longest = values.shape.index(max(values.shape))
    spots = []
    for shift in (0, 1):
        where = [jax.random.randint(jax.random.fold_in(rng, axis), (), 0, length) for axis, length in enumerate(values.shape)]
        where[longest] = (where[longest] + shift) % values.shape[longest]
        spots.append(tuple(where))
    return values.at[spots[0]].set(least).at[spots[1]].set(high)


def block_scale(rng, shape, shards, low, high):
    loudness, own = 1.0, jax.random.fold_in(rng, 6)
    for dim, blocks in shards:
        heights = jnp.exp(jax.random.uniform(jax.random.fold_in(own, dim), (blocks,), jnp.float32, low / len(shards), high / len(shards)))
        loudness = loudness * jnp.repeat(heights, shape[dim] // blocks).reshape([-1 if axis == dim else 1 for axis in range(len(shape))])
    return loudness


def length_profile(number_of, total, reach, lean):
    portions = [(1 << 20) // math.isqrt(rank ** lean) + 1 for rank in range(2, number_of + 1)]
    rest, counts = total - reach - (number_of - 1), [1] * (number_of - 1)
    while rest > 0:
        movable = [i for i in range(number_of - 1) if counts[i] < reach]
        pool, left = sum([portions[i] for i in movable]), rest
        for i in movable:
            extra = min(reach - counts[i], max(1, left * portions[i] // pool), rest)
            counts[i] = counts[i] + extra
            rest = rest - extra
    return np.array([reach] + counts)


def ragged(stream_key, amount, total, most, lean):
    if amount == 2:
        one = jax.random.randint(stream_key, (), max(1, total - most), min(most, total - 1) + 1)
        return jnp.stack([one, total - one])
    tallies = jnp.asarray(length_profile(amount, total, most, lean), jnp.int32)
    twos = (amount - 1) // 2
    giver, receiver = tallies[1:1 + 2 * twos:2], tallies[2:2 + 2 * twos:2]
    room = jnp.minimum(giver - 1, most - receiver)
    passed = jax.random.randint(jax.random.fold_in(stream_key, 1), (twos,), 0, 1 << 20) % (room + 1)
    tallies = tallies.at[1:1 + 2 * twos:2].set(giver - passed).at[2:2 + 2 * twos:2].set(receiver + passed)
    return tallies[jax.random.permutation(jax.random.fold_in(stream_key, 2), amount)]


def deal_out(stream_key, own, number, rows, count, top, bound, lean):
    sequence = jax.random.permutation(stream_key, count)
    crowded, ordinary = load_shares(count, rows * top, bound, lean, True), load_shares(count, rows * top, bound, lean, False)
    places = jnp.arange(count)

    def named(tallies, rotation):
        used = int((tallies > 0).sum())
        fixed = max(1, used // 4)
        moved = fixed + (places - fixed + rotation * (used - fixed)) % max(1, count - fixed)
        return jnp.zeros((count,), jnp.int32).at[sequence[jnp.where(places < fixed, places, moved)]].set(jnp.asarray(tallies, jnp.int32))

    tallies = jnp.where(number % 4 == 0, named(crowded, number // 4), named(ordinary, number - number // 4 - 1))
    mixed = jax.random.permutation(jax.random.fold_in(own, 3), count)
    giver, sink = mixed[0:count // 2 * 2:2], mixed[1:count // 2 * 2:2]
    slack = jnp.minimum(tallies[giver] - 1, bound - tallies[sink]) // 2
    slack = jnp.where((giver == sequence[0]) | (sink == sequence[0]) | (tallies[sink] == 0), 0, jnp.maximum(slack, 0))
    moved = jax.random.randint(jax.random.fold_in(own, 4), (count // 2,), 0, 1 << 20) % (slack + 1)
    tallies = tallies.at[giver].add(-moved).at[sink].add(moved)
    labels = jnp.searchsorted(jnp.cumsum(tallies), jnp.arange(rows * top), side="right").astype(jnp.int32)
    listing = labels.reshape(top, rows).T
    listing = listing[jax.random.permutation(jax.random.fold_in(own, 1), rows)]
    rotation = jax.random.randint(jax.random.fold_in(own, 2), (rows, 1), 0, top)
    return jnp.take_along_axis(listing, (jnp.arange(top)[None, :] + rotation) % top, axis=1)


def load_shares(amount, total, limit, skew, full):
    weights = [(1 << 20) // math.isqrt(standing ** skew) + 1 for standing in range(1, amount + 1)]
    largest = limit if full else min(limit, max(-(-total // amount), total * weights[0] // sum(weights)))
    least = 1 if total - largest >= amount - 1 else 0
    counts, surplus = [largest] + [least] * (amount - 1), total - largest - least * (amount - 1)
    while surplus > 0:
        movable = [i for i in range(1, amount) if counts[i] < largest] or [i for i in range(1, amount) if counts[i] < limit]
        pool, remaining = sum([weights[i] for i in movable]), surplus
        for i in movable:
            addition = min(limit - counts[i], max(1, remaining * weights[i] // pool), surplus)
            counts[i] = counts[i] + addition
            surplus = surplus - addition
    return np.array(counts)


def gaussian(key, extent, deviation, limit, shards=(), kind=jnp.bfloat16):
    loudness = block_scale(key, extent, shards, -0.22, 0.18) if shards else 1.0
    result = jax.random.normal(key, extent, jnp.float32) * deviation * loudness
    return jnp.minimum(jnp.maximum(result, -limit), limit).astype(kind)


def setup_inputs(seed: int = 0) -> dict:
    streams_of = jax.random.split(jax.random.key(seed), 13)
    air_state = gaussian(streams_of[0], (LEVELS, TRACERS, COLS), 1.0, 6.0, ((0, 2), (2, 16)), jnp.float32)
    mix_coef = draw_mix_coef(jax.random.fold_in(streams_of[12], 71), 0)
    flux_scale = jnp.clip(jnp.exp(math.log(4.0) - 2.0794415 * jax.random.uniform(streams_of[2], (COLS,), jnp.float32) ** block_scale(streams_of[2], (COLS,), ((0, 16),), -0.2, 0.2)), 0.5, 4.0)
    sea_state = gaussian(streams_of[3], (TRACERS, SURF), 1.0, 6.0, ((1, 32),), jnp.float32)
    sea_rate = jnp.clip(jnp.exp(math.log(4.0) - 2.0794415 * jax.random.uniform(streams_of[4], (SURF,), jnp.float32) ** block_scale(streams_of[4], (SURF,), ((0, 32),), -0.2, 0.2)), 0.5, 4.0)
    block_counts = jax.vmap(lambda own: ragged(own, BLOCKS_DEV, BLOCKS_DEV * BLOCK_SLOTS * 4 // 5, BLOCK_SLOTS, 2))(jax.random.split(streams_of[5], (N_SECT * N_COLS))).reshape((N_SECT * N_COLS, BLOCKS_DEV)).astype(jnp.int32)
    cell_column = touch_ends(jax.random.randint(streams_of[6], (XCELLS,), 0, BLOCK_COLS), jax.random.fold_in(streams_of[6], 1), 0, BLOCK_COLS - 1).astype(jnp.int32)
    cell_owner_keys = jax.random.split(jax.random.fold_in(streams_of[7], 1), XCELLS // XC_DEV)
    cell_owner_turns = jax.random.permutation(jax.random.fold_in(streams_of[7], 3), XCELLS // XC_DEV)
    cell_owner = jax.vmap(lambda own, number: deal_out(jax.random.fold_in(streams_of[7], 2), own, number, XC_DEV, N_SECT * N_COLS, 1, CAP, 2))(cell_owner_keys, cell_owner_turns).reshape((XCELLS, 1))
    cell_coef = jnp.clip(jnp.exp(math.log(3.0) - 2.3025851 * jax.random.uniform(streams_of[8], (XCELLS,), jnp.float32) ** block_scale(streams_of[8], (XCELLS,), ((0, 32),), -0.2, 0.2)), 0.3, 3.0)
    cell_weight = jnp.clip(jnp.exp(math.log(0.5) - 1.609438 * jax.random.uniform(streams_of[9], (XCELLS,), jnp.float32) ** block_scale(streams_of[9], (XCELLS,), ((0, 32),), -0.2, 0.2)), 0.1, 0.5)
    slot_cell = touch_ends(jax.random.randint(streams_of[10], (RSLOTS,), 0, SC_DEV), jax.random.fold_in(streams_of[10], 1), 0, SC_DEV - 1).astype(jnp.int32)
    slot_frac = jnp.clip(jnp.exp(math.log(1.0) - 1.609438 * jax.random.uniform(streams_of[11], (RSLOTS,), jnp.float32) ** block_scale(streams_of[11], (RSLOTS,), ((0, 32),), -0.2, 0.2)), 0.2, 1.0)
    return dict(air_state=air_state, mix_coef=mix_coef, flux_scale=flux_scale, sea_state=sea_state, sea_rate=sea_rate, block_counts=block_counts, cell_column=cell_column, cell_owner=cell_owner, cell_coef=cell_coef, cell_weight=cell_weight, slot_cell=slot_cell, slot_frac=slot_frac)


def reference(air_state, mix_coef, flux_scale, sea_state, sea_rate, block_counts, cell_column, cell_owner, cell_coef, cell_weight, slot_cell, slot_frac):
    devices = N_SECT * N_COLS

    def level_down(carried, inputs):
        under, upper_part = carried
        coupling, column_values = inputs
        denom = 1.0 + coupling + under
        part = (column_values + upper_part) / denom
        ratio = coupling / denom
        return (coupling * (1.0 - ratio), coupling * part), (part, denom)

    start = (jnp.zeros((COLS,), jnp.float32), jnp.zeros((TRACERS, COLS), jnp.float32))
    _, (parts, denoms) = lax.scan(level_down, start, (mix_coef, air_state))
    ratios = mix_coef / denoms
    resid = parts[-1]
    slope = flux_scale / denoms[-1]

    slots = jnp.arange(XCELLS, dtype=jnp.int32)
    device = slots // XC_DEV
    local = slots % XC_DEV
    block = local // BLOCK_SLOTS
    within = local % BLOCK_SLOTS
    live = (within < block_counts[device, block]).astype(jnp.float32)
    column = (device % N_COLS) * COL_DEV + block * BLOCK_COLS + cell_column
    owner = cell_owner[:, 0]

    def ranks_of(owners):
        onehot = (owners[:, None] == jnp.arange(devices, dtype=jnp.int32)[None, :]).astype(jnp.int32)
        return jnp.sum(jnp.cumsum(onehot, axis=0) * onehot, axis=1) - 1

    ranks = lax.map(ranks_of, owner.reshape(devices, XC_DEV)).reshape(XCELLS).astype(jnp.int32)
    arrive = owner * RECV + device * CAP + ranks
    surface_cell = owner * SC_DEV + slot_cell[arrive]
    fraction = slot_frac[arrive]
    gain = cell_coef * live
    coupling_cell = gain * fraction

    flux_col = jnp.zeros((TRACERS, COLS), jnp.float32)
    sea = sea_state
    for step in range(SUBSTEPS):
        bottom = resid + slope * flux_col
        at_cells = bottom[:, column]
        numer = jnp.zeros((TRACERS, SURF), jnp.float32).at[:, surface_cell].add(coupling_cell * at_cells)
        total = jnp.zeros((SURF,), jnp.float32).at[surface_cell].add(coupling_cell)
        sea = (sea + sea_rate * numer) / (1.0 + sea_rate * total)
        flux = cell_weight * gain * (sea[:, surface_cell] - at_cells)
        flux_col = jnp.zeros((TRACERS, COLS), jnp.float32).at[:, column].add(flux)
    bottom = resid + slope * flux_col

    def level_up(below, inputs):
        part, ratio = inputs
        value = part + ratio * below
        return value, value

    _, rising = lax.scan(level_up, bottom, (parts[:-1], ratios[:-1]), reverse=True)
    air_new = jnp.concatenate([rising, bottom[None]], axis=0)
    return air_new, sea
```

```python
import functools

import jax
import jax.numpy as jnp
from jax import lax
from jax.experimental import pallas as pl
from jax.experimental.pallas import tpu as pltpu
from jax.sharding import PartitionSpec as P

BLOCK_COLS = 128
BLOCK_SLOTS = 256
SUBSTEPS = 2
LANES = 128
COL_TILE = 1024
PARAMS = pltpu.CompilerParams(vmem_limit_bytes=40 * 1024 * 1024)


def split(value):
    high = value.astype(jnp.bfloat16).astype(jnp.float32)
    return high, value - high


def hot(index, count):
    places = lax.broadcasted_iota(jnp.int32, (count, index.shape[1]), 0).astype(jnp.int16)
    return jnp.where(places == index.astype(jnp.int16), jnp.ones((), jnp.bfloat16), jnp.zeros((), jnp.bfloat16))


def in_line(packed):
    return jnp.concatenate([packed[r : r + 1] for r in range(packed.shape[0])], axis=1)


def in_rows(line):
    return jnp.concatenate([line[:, r : r + LANES] for r in range(0, line.shape[1], LANES)], axis=0)


def scatter(values, row, lane, rows):
    mask = hot(row, rows)
    parts = [split(value) for value in values]
    lines = [in_line(p[0]) for p in parts] + [in_line(p[1]) for p in parts]
    return lax.dot_general(
        jnp.concatenate([mask * line.astype(jnp.bfloat16) for line in lines], axis=0),
        hot(lane, LANES),
        (((1,), (1,)), ((), ())),
        preferred_element_type=jnp.float32,
    )


def table_of(value):
    high, low = split(value)
    return jnp.concatenate([high, low], axis=1).astype(jnp.bfloat16)


def gather(table, row, lane, rows):
    lane_hot = hot(lane, LANES)
    picked = jnp.dot(table, jnp.concatenate([lane_hot, lane_hot], axis=0), preferred_element_type=jnp.float32)
    mask = lax.broadcasted_iota(jnp.int32, (rows, row.shape[1]), 0) == row
    return [
        jnp.sum(jnp.where(mask, picked[q : q + rows], 0.0), axis=0, keepdims=True)
        for q in range(0, table.shape[0], rows)
    ]


def setup_kernel(devices, cap_rows, step, owner, column, coef, weight, counts, out, acc, offset):
    ring = devices // 2
    slots = step * LANES
    blocks = slots // BLOCK_SLOTS
    acc[...] = jnp.zeros_like(acc)
    offset[...] = jnp.zeros_like(offset)
    later = (
        lax.broadcasted_iota(jnp.int32, (BLOCK_SLOTS, BLOCK_SLOTS), 0)
        <= lax.broadcasted_iota(jnp.int32, (BLOCK_SLOTS, BLOCK_SLOTS), 1)
    )
    later = jnp.where(later, 1.0, 0.0).astype(jnp.bfloat16)
    places = devices * cap_rows
    numbers = lax.broadcasted_iota(jnp.int32, (step, LANES), 0)
    within = lax.rem(numbers, 2) * LANES + lax.broadcasted_iota(jnp.int32, (step, LANES), 1)

    def part(i, _):
        here = pl.ds(pl.multiple_of(i * step, step), step)
        own_packed = owner[here, :]
        own = in_line(own_packed)
        named = hot(own, devices)
        named_blocks = [named[:, b * BLOCK_SLOTS : (b + 1) * BLOCK_SLOTS] for b in range(blocks)]
        running = jnp.dot(jnp.concatenate(named_blocks, axis=0), later, preferred_element_type=jnp.float32)
        before = offset[...]
        ranks = []
        for b in range(blocks):
            wide = named_blocks[b].astype(jnp.float32)
            count = running[b * devices : (b + 1) * devices] + before[:, 0:1]
            ranks.append(jnp.sum(wide * count, axis=0, keepdims=True) - 1.0)
            before = before + jnp.broadcast_to(jnp.sum(wide, axis=1, keepdims=True), before.shape)
        offset[...] = before
        rank = jnp.concatenate(ranks, axis=1).astype(jnp.int32)
        gain = jnp.where(within < counts[here, :], coef[here, :], 0.0)
        flow = weight[here, :] * gain
        gain_high, gain_low = split(gain)
        flow_high, flow_low = split(flow)
        values = [
            ((i * step + numbers) // 2).astype(jnp.float32),
            column[here, :].astype(jnp.float32),
            gain_high,
            gain_low,
            flow_high,
            flow_low,
        ]
        row = (lax.rem(own, ring) * 2 + own // ring) * cap_rows + rank // LANES
        mask = hot(row, places)
        acc[...] += lax.dot_general(
            jnp.concatenate([mask * in_line(value).astype(jnp.bfloat16) for value in values], axis=0),
            hot(lax.rem(rank, LANES), LANES),
            (((1,), (1,)), ((), ())),
            preferred_element_type=jnp.float32,
        )
        return 0

    lax.fori_loop(0, owner.shape[0] // step, part, 0)
    out[0] = acc[0:places]
    out[1] = acc[places : 2 * places]
    out[2] = acc[2 * places : 3 * places] + acc[3 * places : 4 * places]
    out[3] = acc[4 * places : 5 * places] + acc[5 * places : 6 * places]


def setup(owner, column, coef, weight, counts, devices, cap_rows):
    places = devices * cap_rows
    step = max(2, min(16, 2048 // places))
    while owner.shape[0] % step:
        step -= 2
    return pl.pallas_call(
        functools.partial(setup_kernel, devices, cap_rows, step),
        out_shape=jax.ShapeDtypeStruct((4, places, LANES), jnp.float32),
        scratch_shapes=[
            pltpu.VMEM((6 * places, LANES), jnp.float32),
            pltpu.VMEM((devices, LANES), jnp.float32),
        ],
        compiler_params=PARAMS,
    )(owner, column, coef, weight, counts)


def level_down(mix, air, k, under, carried):
    coupling = mix[k : k + 1, :]
    inverse = 1.0 / (1.0 + coupling + under)
    part = (air[k] + carried) * inverse
    ratio = coupling * inverse
    return part, ratio, inverse, ratio * (1.0 + under), coupling * part


def descend_end_kernel(air, mix, end):
    under = jnp.zeros((1, end.shape[1]), jnp.float32)
    carried = jnp.zeros((air.shape[0], end.shape[1]), jnp.float32)
    levels_first = jnp.swapaxes(air[...], 0, 1)
    for k in range(air.shape[1]):
        _, _, _, under, carried = level_down(mix, levels_first, k, under, carried)
    end[...] = jnp.concatenate([carried, under], axis=0)


def descend_end(air, mix):
    tracers, levels, columns = air.shape
    return pl.pallas_call(
        descend_end_kernel,
        grid=(columns // COL_TILE,),
        in_specs=[
            pl.BlockSpec((tracers, levels, COL_TILE), lambda j: (0, 0, j)),
            pl.BlockSpec((levels, COL_TILE), lambda j: (0, j)),
        ],
        out_specs=pl.BlockSpec((tracers + 1, COL_TILE), lambda j: (0, j)),
        out_shape=jax.ShapeDtypeStruct((tracers + 1, columns), jnp.float32),
        compiler_params=PARAMS,
    )(air, mix)


def descend_kernel(air, mix, start, last, parts, ratios, ends):
    tracers, levels, _ = air.shape
    levels_first = jnp.swapaxes(air[...], 0, 1)
    carried = start[0:tracers, :]
    under = start[tracers : tracers + 1, :]
    for k in range(levels):
        part, ratio, inverse, under, carried = level_down(mix, levels_first, k, under, carried)
        parts[k] = part
        if k == levels - 1:
            ratio = last[...] * inverse
        ratios[k : k + 1, :] = ratio
    value, factor = part, ratio
    ends[0, 0:tracers, :] = part
    ends[0, tracers : tracers + 1, :] = ratio
    for k in range(levels - 2, -1, -1):
        ratio = ratios[k : k + 1, :]
        value = parts[k] + ratio * value
        factor = ratio * factor
    ends[1, 0:tracers, :] = value
    ends[1, tracers : tracers + 1, :] = factor


def descend(air, mix, start, last):
    tracers, levels, columns = air.shape
    return pl.pallas_call(
        descend_kernel,
        grid=(columns // COL_TILE,),
        in_specs=[
            pl.BlockSpec((tracers, levels, COL_TILE), lambda j: (0, 0, j)),
            pl.BlockSpec((levels, COL_TILE), lambda j: (0, j)),
            pl.BlockSpec((tracers + 1, COL_TILE), lambda j: (0, j)),
            pl.BlockSpec((1, COL_TILE), lambda j: (0, j)),
        ],
        out_specs=[
            pl.BlockSpec((levels, tracers, COL_TILE), lambda j: (0, 0, j)),
            pl.BlockSpec((levels, COL_TILE), lambda j: (0, j)),
            pl.BlockSpec((2, tracers + 1, COL_TILE), lambda j: (0, 0, j)),
        ],
        out_shape=[
            jax.ShapeDtypeStruct((levels, tracers, columns), jnp.float32),
            jax.ShapeDtypeStruct(mix.shape, jnp.float32),
            jax.ShapeDtypeStruct((2, tracers + 1, columns), jnp.float32),
        ],
        compiler_params=PARAMS,
    )(air, mix, start, last)


def ascend_kernel(parts, ratios, below, out):
    value = below[...]
    risen = []
    for k in range(parts.shape[0] - 1, -1, -1):
        value = parts[k] + ratios[k : k + 1, :] * value
        risen.append(value)
    out[...] = jnp.swapaxes(jnp.stack(risen[::-1]), 0, 1)


def ascend(parts, ratios, below):
    levels, tracers, columns = parts.shape
    return pl.pallas_call(
        ascend_kernel,
        grid=(columns // COL_TILE,),
        in_specs=[
            pl.BlockSpec((levels, tracers, COL_TILE), lambda j: (0, 0, j)),
            pl.BlockSpec((levels, COL_TILE), lambda j: (0, j)),
            pl.BlockSpec((tracers, COL_TILE), lambda j: (0, j)),
        ],
        out_specs=pl.BlockSpec((tracers, levels, COL_TILE), lambda j: (0, 0, j)),
        out_shape=jax.ShapeDtypeStruct((tracers, levels, columns), jnp.float32),
        compiler_params=PARAMS,
    )(parts, ratios, below)


def exchange_kernel(
    tracers,
    ring,
    cap_rows,
    resid,
    slope,
    sorted_cells,
    surface,
    sea,
    rate,
    flux_out,
    sea_out,
    cells,
    spots,
    waters,
    rates,
    col_row,
    col_lane,
    flow,
    gain_sent,
    gain_came,
    strength,
    inverse,
    flux,
    sent,
    arrived,
    back,
    returned,
    acc,
    total,
    send_sem,
    recv_sem,
    pair_send,
    pair_recv,
    local_sem,
):
    rows, surf_rows = slope.shape[0], rate.shape[0]
    mine = tracers // 2
    half = 2 * cap_rows
    whole = 2 * half
    sect = lax.axis_index("sect")
    me = lax.axis_index("cols")
    other = 1 - sect

    def ahead(s):
        return lax.rem(me + s, ring)

    def behind(s):
        return lax.rem(me + ring - s, ring)

    def to(phase, source, target, s):
        return pltpu.make_async_remote_copy(
            src_ref=source.at[ahead(s)],
            dst_ref=target.at[me],
            send_sem=send_sem.at[phase, s],
            recv_sem=recv_sem.at[phase, s],
            device_id=(sect, ahead(s)),
            device_id_type=pl.DeviceIdType.MESH,
        )

    def to_partner(k, source, target):
        return pltpu.make_async_remote_copy(
            src_ref=source,
            dst_ref=target,
            send_sem=pair_send.at[k],
            recv_sem=pair_recv.at[k],
            device_id=(other, me),
            device_id_type=pl.DeviceIdType.MESH,
        )

    def in_pairs(act):
        def far(i, _):
            act(ring // 2 + 2 * i, ring // 2 + 2 * i + 1)
            return 0

        def near(i, _):
            act(ring // 2 - 1 - 2 * i, ring // 2 - 2 - 2 * i)
            return 0

        lax.fori_loop(0, ring // 4, far, 0)
        lax.fori_loop(0, ring // 4 - 1, near, 0)
        act(1, 0)

    barrier = pltpu.get_barrier_semaphore()

    def greet(s, _):
        pl.semaphore_signal(barrier, inc=1, device_id=(sect, ahead(s)), device_id_type=pl.DeviceIdType.MESH)
        return 0

    lax.fori_loop(1, ring, greet, 0)
    pl.semaphore_signal(barrier, inc=1, device_id=(other, me), device_id_type=pl.DeviceIdType.MESH)
    pl.semaphore_wait(barrier, ring)

    their_sea = sea.at[pl.ds(pl.multiple_of(other * (mine * surf_rows), 8), mine * surf_rows)]
    my_sea = sea.at[pl.ds(pl.multiple_of(sect * (mine * surf_rows), 8), mine * surf_rows)]
    shared = [
        to_partner(0, sorted_cells, cells.at[sect]),
        to_partner(1, surface, spots.at[sect]),
        to_partner(2, their_sea, waters.at[sect]),
        to_partner(3, rate, rates.at[sect]),
    ]
    kept = [
        pltpu.make_async_copy(sorted_cells, cells.at[sect], local_sem.at[0]),
        pltpu.make_async_copy(surface, spots.at[sect], local_sem.at[1]),
        pltpu.make_async_copy(my_sea, waters.at[sect], local_sem.at[2]),
        pltpu.make_async_copy(rate, rates.at[sect], local_sem.at[3]),
    ]
    for copy in shared + kept:
        copy.start()
    flux[...] = jnp.zeros_like(flux)
    for copy in kept:
        copy.wait()
    for copy in shared:
        copy.wait()

    def arrange(chip, _):
        here = pl.ds(pl.multiple_of(chip * half, 8), half)

        def merged(v):
            upper, lower = cells[0, v, here, :], cells[1, v, here, :]
            return jnp.concatenate(
                [upper[0:cap_rows], lower[0:cap_rows], upper[cap_rows:], lower[cap_rows:]], axis=0
            )

        col_row[chip] = merged(0).astype(jnp.int32)
        col_lane[chip] = merged(1).astype(jnp.int32)
        gain_sent[chip] = merged(2)
        flow[chip] = merged(3)
        return 0

    lax.fori_loop(0, ring, arrange, 0)

    def send_gain(s, _):
        to(0, gain_sent, gain_came, s).start()
        return 0

    lax.fori_loop(1, ring, send_gain, 0)
    gain_came[me] = gain_sent[me]
    my_resid = resid.at[pl.ds(pl.multiple_of(sect * (mine * rows), 8), mine * rows)]

    def spot(v, d, chips):
        return in_line(
            jnp.concatenate(
                [spots[d, v, pl.ds(pl.multiple_of(chip * half, 8), half), :] for chip in chips], axis=0
            )
        ).astype(jnp.int32)

    for step in range(SUBSTEPS):
        out_phase, back_phase = 1 + 2 * step, 2 + 2 * step
        bottom = my_resid[...] + jnp.concatenate([slope[...]] * mine, axis=0) * flux[...]
        table = table_of(bottom)

        def send(*steps):
            chips = [ahead(s) for s in steps]
            row = in_line(jnp.concatenate([col_row[chip] for chip in chips], axis=0))
            lane = in_line(jnp.concatenate([col_lane[chip] for chip in chips], axis=0))
            picked = [in_rows(p) for p in gather(table, row, lane, rows)]
            for j, (s, chip) in enumerate(zip(steps, chips)):
                for q in range(mine):
                    sent[chip, q * whole : (q + 1) * whole, :] = picked[q][j * whole : (j + 1) * whole]
                if not (isinstance(s, int) and s == 0):
                    to(out_phase, sent, arrived, s).start()

        in_pairs(send)
        arrived[me] = sent[me]
        acc[...] = jnp.zeros_like(acc)
        if step == 0:
            total[...] = jnp.zeros_like(total)

        def receive(*steps):
            chips = [behind(s) for s in steps]
            for s in steps:
                if not (isinstance(s, int) and s == 0):
                    if step == 0:
                        to(0, gain_sent, gain_came, s).wait_recv()
                    to(out_phase, sent, arrived, s).wait_recv()
            for d in range(2):
                row, lane = spot(0, d, chips), spot(1, d, chips)
                force = []
                for chip in chips:
                    if step == 0:
                        frac = spots[d, 2, pl.ds(pl.multiple_of(chip * half, 8), half), :]
                        strength[chip, d * half : (d + 1) * half, :] = (
                            gain_came[chip, d * half : (d + 1) * half, :] * frac
                        )
                    force.append(strength[chip, d * half : (d + 1) * half, :])
                values = [
                    jnp.concatenate(
                        [
                            arrived[chip, q * whole + d * half : q * whole + (d + 1) * half, :] * f
                            for chip, f in zip(chips, force)
                        ],
                        axis=0,
                    )
                    for q in range(mine)
                ]
                if step == 0:
                    values.append(jnp.concatenate(force, axis=0))
                summed = scatter(values, row, lane, surf_rows)
                span = len(values) * surf_rows
                wide = mine * surf_rows
                acc[d] += summed[0:wide] + summed[span : span + wide]
                if step == 0:
                    total[d] += summed[wide:span] + summed[span + wide :]

        in_pairs(receive)
        for d in range(2):
            if step == 0:
                inverse[d] = 1.0 / (1.0 + rates[d] * total[d])
            for q in range(mine):
                here = slice(q * surf_rows, (q + 1) * surf_rows)
                waters[d, here, :] = (waters[d, here, :] + rates[d] * acc[d, here, :]) * inverse[d]
        tables = [table_of(waters[d]) for d in range(2)]
        if step == 1:
            pass

        def give_back(*steps):
            chips = [ahead(s) for s in steps]
            for d in range(2):
                picked = [in_rows(p) for p in gather(tables[d], spot(0, d, chips), spot(1, d, chips), surf_rows)]
                for j, chip in enumerate(chips):
                    for q in range(mine):
                        back[chip, q * whole + d * half : q * whole + (d + 1) * half, :] = picked[q][
                            j * half : (j + 1) * half
                        ]
            for s in steps:
                if not (isinstance(s, int) and s == 0):
                    to(back_phase, back, returned, s).start()

        in_pairs(give_back)
        returned[me] = back[me]
        flux[...] = jnp.zeros_like(flux)

        def take_back(*steps):
            chips = [behind(s) for s in steps]
            for s in steps:
                if not (isinstance(s, int) and s == 0):
                    to(back_phase, back, returned, s).wait_recv()
            values = []
            for q in range(mine):
                here = slice(q * whole, (q + 1) * whole)
                values.append(
                    jnp.concatenate(
                        [(returned[chip, here, :] - sent[chip, here, :]) * flow[chip] for chip in chips], axis=0
                    )
                )
            row = in_line(jnp.concatenate([col_row[chip] for chip in chips], axis=0))
            lane = in_line(jnp.concatenate([col_lane[chip] for chip in chips], axis=0))
            summed = scatter(values, row, lane, rows)
            flux[...] += summed[0 : mine * rows] + summed[mine * rows :]

        in_pairs(take_back)

        def finish(s, _):
            if step == 0:
                to(0, gain_sent, gain_came, s).wait_send()
            to(out_phase, sent, arrived, s).wait_send()
            to(back_phase, back, returned, s).wait_send()
            return 0

        lax.fori_loop(1, ring, finish, 0)

    flux_here = flux_out.at[pl.ds(pl.multiple_of(sect * (mine * rows), 8), mine * rows)]
    sea_here = sea_out.at[pl.ds(pl.multiple_of(sect * (mine * surf_rows), 8), mine * surf_rows)]
    last = [
        to_partner(4, flux, flux_here),
        to_partner(5, waters.at[other], sea_here),
    ]
    stay = [
        pltpu.make_async_copy(flux, flux_here, local_sem.at[4]),
        pltpu.make_async_copy(waters.at[sect], sea_here, local_sem.at[5]),
    ]
    for copy in last + stay:
        copy.start()
    for copy in last + stay:
        copy.wait()


def exchange(tracers, ring, cap_rows, resid, slope, sorted_cells, surface, sea, rate):
    rows, surf_rows = slope.shape[0], rate.shape[0]
    mine = tracers // 2
    whole = 4 * cap_rows
    real = lambda *shape: pltpu.VMEM(shape, jnp.float32)
    message = real(ring, mine * whole, LANES)
    once = real(ring, whole, LANES)
    return pl.pallas_call(
        functools.partial(exchange_kernel, tracers, ring, cap_rows),
        out_shape=[
            jax.ShapeDtypeStruct(resid.shape, jnp.float32),
            jax.ShapeDtypeStruct(sea.shape, jnp.float32),
        ],
        in_specs=[pl.BlockSpec(memory_space=pltpu.VMEM)] * 6,
        out_specs=[pl.BlockSpec(memory_space=pltpu.VMEM)] * 2,
        scratch_shapes=[
            real(2, *sorted_cells.shape),
            real(2, *surface.shape),
            real(2, mine * surf_rows, LANES),
            real(2, surf_rows, LANES),
            pltpu.VMEM((ring, whole, LANES), jnp.int32),
            pltpu.VMEM((ring, whole, LANES), jnp.int32),
            once,
            once,
            once,
            once,
            real(2, surf_rows, LANES),
            real(mine * rows, LANES),
            message,
            message,
            message,
            message,
            real(2, mine * surf_rows, LANES),
            real(2, surf_rows, LANES),
            pltpu.SemaphoreType.DMA((1 + 2 * SUBSTEPS, ring)),
            pltpu.SemaphoreType.DMA((1 + 2 * SUBSTEPS, ring)),
            pltpu.SemaphoreType.DMA((6,)),
            pltpu.SemaphoreType.DMA((6,)),
            pltpu.SemaphoreType.DMA((6,)),
        ],
        compiler_params=pltpu.CompilerParams(
            vmem_limit_bytes=40 * 1024 * 1024, collective_id=0, has_side_effects=True
        ),
    )(resid, slope, sorted_cells, surface, sea, rate)


def body(
    air_state,
    mix_coef,
    flux_scale,
    sea_state,
    sea_rate,
    block_counts,
    cell_column,
    cell_owner,
    cell_coef,
    cell_weight,
    slot_cell,
    slot_frac,
):
    levels, tracers, columns = air_state.shape
    is_lower = lax.axis_index("sect") == 1
    ring = lax.axis_size("cols")
    devices = 2 * ring
    rows = columns // BLOCK_COLS
    surf_cells = sea_state.shape[1]
    surf_rows = surf_cells // LANES
    capacity = slot_cell.shape[0] // devices
    cap_rows = max(4, -(-capacity // LANES))

    air = jnp.swapaxes(air_state, 0, 1)
    handed = lax.ppermute(descend_end(air, mix_coef), "sect", [(0, 1)])
    sorted_cells = setup(
        cell_owner.reshape(-1, LANES),
        cell_column.reshape(-1, LANES),
        cell_coef.reshape(-1, LANES),
        cell_weight.reshape(-1, LANES),
        jnp.broadcast_to(block_counts.reshape(-1, 1, 1), (rows, 2, LANES)).reshape(-1, LANES),
        devices,
        cap_rows,
    )

    def by_chip(values):
        values = jnp.pad(values.reshape(2, ring, capacity), ((0, 0), (0, 0), (0, cap_rows * LANES - capacity)))
        values = jnp.swapaxes(values.reshape(2, ring, cap_rows, LANES), 0, 1)
        return values.reshape(ring * 2 * cap_rows, LANES)

    cell = by_chip(slot_cell)
    surface = jnp.stack(
        [(cell // LANES).astype(jnp.float32), (cell % LANES).astype(jnp.float32), by_chip(slot_frac)]
    )

    last = jnp.where(is_lower, flux_scale, mix_coef[-1])[None]
    parts, ratios, ends = descend(air, mix_coef, handed, last)
    received = lax.ppermute(ends, "sect", [(1, 0)])
    low = jnp.where(is_lower, ends, received)
    resid = low[0, :tracers].reshape(tracers * rows, LANES)
    slope = low[0, tracers].reshape(rows, LANES)

    flux, sea = exchange(
        tracers,
        ring,
        cap_rows,
        resid,
        slope,
        sorted_cells,
        surface,
        sea_state.reshape(tracers * surf_rows, LANES),
        sea_rate.reshape(surf_rows, LANES),
    )
    flux_col = flux.reshape(tracers, columns)
    below = jnp.where(is_lower, flux_col, low[1, :tracers] + low[1, tracers] * flux_col)
    return (jnp.swapaxes(ascend(parts, ratios, below), 0, 1), sea.reshape(tracers, surf_cells))


def solution(mesh):
    return jax.shard_map(
        body,
        mesh=mesh,
        in_specs=(
            P("sect", None, "cols"),
            P("sect", "cols"),
            P("cols"),
            P(None, ("sect", "cols")),
            P(("sect", "cols")),
            P(("sect", "cols"), None),
            P(("sect", "cols")),
            P(("sect", "cols"), None),
            P(("sect", "cols")),
            P(("sect", "cols")),
            P(("sect", "cols")),
            P(("sect", "cols")),
        ),
        out_specs=(P("sect", None, "cols"), P(None, ("sect", "cols"))),
        check_vma=False,
    )
```

```python
import functools

import jax
import jax.numpy as jnp
from jax import lax
from jax.experimental import pallas as pl
from jax.experimental.pallas import tpu as pltpu
from jax.sharding import PartitionSpec as P

BLOCK_COLS = 128
BLOCK_SLOTS = 256
SUBSTEPS = 2
GROUPS = 2
LANES = 128
VMEM = pl.BlockSpec(memory_space=pltpu.VMEM)
HBM = pl.BlockSpec(memory_space=pltpu.HBM)


def split(value):
    high = value.astype(jnp.bfloat16).astype(jnp.float32)
    return high, value - high


def hot(index, count):
    places = lax.broadcasted_iota(jnp.int32, (count, index.shape[1]), 0).astype(jnp.int16)
    return jnp.where(places == index.astype(jnp.int16), jnp.ones((), jnp.bfloat16), jnp.zeros((), jnp.bfloat16))


def in_line(packed):
    return jnp.concatenate([packed[r : r + 1] for r in range(packed.shape[0])], axis=1)


def in_rows(line):
    return jnp.concatenate([line[:, r : r + LANES] for r in range(0, line.shape[1], LANES)], axis=0)


def scatter(values, row, lane, rows):
    mask = hot(row, rows)
    parts = [split(value) for value in values]
    lines = [in_line(p[0]) for p in parts] + [in_line(p[1]) for p in parts]
    return lax.dot_general(
        jnp.concatenate([mask * line.astype(jnp.bfloat16) for line in lines], axis=0),
        hot(lane, LANES),
        (((1,), (1,)), ((), ())),
        preferred_element_type=jnp.float32,
    )


def table_of(value):
    high, low = split(value)
    return jnp.concatenate([high, low], axis=1).astype(jnp.bfloat16)


def gather(table, row, lane, rows):
    lane_hot = hot(lane, LANES)
    picked = jnp.dot(table, jnp.concatenate([lane_hot, lane_hot], axis=0), preferred_element_type=jnp.float32)
    mask = lax.broadcasted_iota(jnp.int32, (rows, row.shape[1]), 0) == row
    return [
        jnp.sum(jnp.where(mask, picked[q : q + rows], 0.0), axis=0, keepdims=True)
        for q in range(0, table.shape[0], rows)
    ]


def forward_kernel(
    tracers,
    ring,
    cap_rows,
    step_rows,
    air,
    mix,
    scale,
    owner,
    column,
    coef,
    weight,
    counts,
    spots,
    sea,
    rate,
    parts,
    ratios,
    below,
    sea_out,
    mixes,
    inverses,
    hand,
    low,
    top,
    place_acc,
    offset,
    sorted_cells,
    cells,
    col_row,
    col_lane,
    flow,
    gain_sent,
    gain_came,
    strength,
    inverse,
    sent,
    arrived,
    back,
    returned,
    flux,
    flux_came,
    acc,
    send_sem,
    recv_sem,
    pair_send,
    pair_recv,
    local_sem,
    load_sem,
):
    levels, rows = ratios.shape[0], ratios.shape[1]
    surf_rows = rate.shape[0]
    devices = 2 * ring
    mine = tracers // GROUPS
    spot_rows = 2 * cap_rows
    sect = lax.axis_index("sect")
    me = lax.axis_index("cols")
    other = 1 - sect

    def ahead(s):
        return lax.rem(me + s, ring)

    def behind(s):
        return lax.rem(me + ring - s, ring)

    def remote(s):
        return not (isinstance(s, int) and s == 0)

    def to(phase, source, target, s):
        return pltpu.make_async_remote_copy(
            src_ref=source.at[ahead(s)],
            dst_ref=target.at[me],
            send_sem=send_sem.at[phase, s],
            recv_sem=recv_sem.at[phase, s],
            device_id=(sect, ahead(s)),
            device_id_type=pl.DeviceIdType.MESH,
        )

    def outward(step, g, s):
        return to(1 + 2 * (step * GROUPS + g), sent.at[g], arrived.at[g], s)

    def homeward(step, g, s):
        return to(2 + 2 * (step * GROUPS + g), back.at[g], returned.at[g], s)

    def to_partner(k, source, target):
        return pltpu.make_async_remote_copy(
            src_ref=source,
            dst_ref=target,
            send_sem=pair_send.at[k],
            recv_sem=pair_recv.at[k],
            device_id=(other, me),
            device_id_type=pl.DeviceIdType.MESH,
        )

    def flux_over(step, g):
        return to_partner(1 + step * GROUPS + g, flux.at[step, g], flux_came.at[step, g])

    def in_fours(act):
        def far(i, _):
            act(*[ring // 2 + 4 * i + j for j in range(4)])
            return 0

        def near(i, _):
            act(*[ring // 2 - 1 - 4 * i - j for j in range(4)])
            return 0

        lax.fori_loop(0, ring // 8, far, 0)
        lax.fori_loop(0, ring // 8 - 1, near, 0)
        act(3, 2, 1, 0)

    def line_of(ref, chips):
        return in_line(jnp.concatenate([ref[chip] for chip in chips], axis=0))

    def spot(v, chips):
        return in_line(
            jnp.concatenate(
                [spots[v, pl.ds(pl.multiple_of(chip * spot_rows, 8), spot_rows), :] for chip in chips], axis=0
            )
        ).astype(jnp.int32)

    barrier = pltpu.get_barrier_semaphore()

    def greet(s, _):
        pl.semaphore_signal(barrier, inc=1, device_id=(sect, ahead(s)), device_id_type=pl.DeviceIdType.MESH)
        return 0

    lax.fori_loop(1, ring, greet, 0)
    pl.semaphore_signal(barrier, inc=1, device_id=(other, me), device_id_type=pl.DeviceIdType.MESH)

    def load(j):
        here = pl.ds(pl.multiple_of(j * LANES, LANES), LANES)
        return [
            pltpu.make_async_copy(mix.at[:, here], mixes.at[:, j, :], load_sem.at[0, j]),
            pltpu.make_async_copy(air.at[:, :, here], parts.at[:, :, j, :], load_sem.at[1, j]),
        ]

    def start_load(j, _):
        for copy in load(j):
            copy.start()
        return 0

    def wait_load(j, _):
        for copy in load(j):
            copy.wait()
        return 0

    lax.fori_loop(0, rows, start_load, 0)

    places = devices * cap_rows
    blocks = step_rows * LANES // BLOCK_SLOTS
    place_acc[...] = jnp.zeros_like(place_acc)
    offset[...] = jnp.zeros_like(offset)
    later = (
        lax.broadcasted_iota(jnp.int32, (BLOCK_SLOTS, BLOCK_SLOTS), 0)
        <= lax.broadcasted_iota(jnp.int32, (BLOCK_SLOTS, BLOCK_SLOTS), 1)
    )
    later = jnp.where(later, 1.0, 0.0).astype(jnp.bfloat16)
    numbers = lax.broadcasted_iota(jnp.int32, (step_rows, LANES), 0)
    within = lax.rem(numbers, 2) * LANES + lax.broadcasted_iota(jnp.int32, (step_rows, LANES), 1)

    def sort_part(i, _):
        here = pl.ds(pl.multiple_of(i * step_rows, step_rows), step_rows)
        own = in_line(owner[here, :])
        named = hot(own, devices)
        named_blocks = [named[:, b * BLOCK_SLOTS : (b + 1) * BLOCK_SLOTS] for b in range(blocks)]
        running = jnp.dot(jnp.concatenate(named_blocks, axis=0), later, preferred_element_type=jnp.float32)
        before = offset[...]
        ranks = []
        for b in range(blocks):
            wide = named_blocks[b].astype(jnp.float32)
            count = running[b * devices : (b + 1) * devices] + before[:, 0:1]
            ranks.append(jnp.sum(wide * count, axis=0, keepdims=True) - 1.0)
            before = before + jnp.broadcast_to(jnp.sum(wide, axis=1, keepdims=True), before.shape)
        offset[...] = before
        rank = jnp.concatenate(ranks, axis=1).astype(jnp.int32)
        gain = jnp.where(within < counts[here, :], coef[here, :], 0.0)
        gain_high, gain_low = split(gain)
        flow_high, flow_low = split(weight[here, :] * gain)
        values = [
            ((i * step_rows + numbers) // 2).astype(jnp.float32),
            column[here, :].astype(jnp.float32),
            gain_high,
            gain_low,
            flow_high,
            flow_low,
        ]
        mask = hot(own * cap_rows + rank // LANES, places)
        place_acc[...] += lax.dot_general(
            jnp.concatenate([mask * in_line(value).astype(jnp.bfloat16) for value in values], axis=0),
            hot(lax.rem(rank, LANES), LANES),
            (((1,), (1,)), ((), ())),
            preferred_element_type=jnp.float32,
        )
        return 0

    def eliminate(under):
        def coefficients(k, under):
            coupling = mixes[k]
            inv = 1.0 / (1.0 + coupling + under)
            ratio = coupling * inv
            inverses[k] = inv
            ratios[k] = ratio
            return ratio * (1.0 + under)

        return lax.fori_loop(0, levels, coefficients, under, unroll=4)

    def descend(carried_of, keep):
        for q in range(0, tracers, 2):

            def level(k, carried):
                ratio, inv = ratios[k], inverses[k]
                result = []
                for j, value in enumerate(carried):
                    value = parts[q + j, k] + value
                    parts[q + j, k] = value * inv
                    result.append(value * ratio)
                return result

            keep(q, lax.fori_loop(0, levels, level, [carried_of(q), carried_of(q + 1)], unroll=4))

    handed = to_partner(1 + SUBSTEPS * GROUPS, hand, hand)
    lowest = to_partner(2 + SUBSTEPS * GROUPS, low, low)
    highest = to_partner(3 + SUBSTEPS * GROUPS, top, top)
    upper, lower = sect == 0, sect == 1

    def piece(q):
        return slice(q * rows, (q + 1) * rows)

    sort_steps = owner.shape[0] // step_rows
    early = sort_steps // 3
    lax.fori_loop(0, early, sort_part, 0)
    pl.semaphore_wait(barrier, ring)
    lax.fori_loop(0, rows, wait_load, 0)

    @pl.when(upper)
    def _():
        zero = jnp.zeros((rows, LANES), jnp.float32)
        hand[piece(tracers), :] = eliminate(zero)

        def keep(q, carried):
            hand[piece(q), :] = carried[0]
            hand[piece(q + 1), :] = carried[1]

        descend(lambda q: zero, keep)
        handed.start()

    lax.fori_loop(early, sort_steps, sort_part, 0)
    for v in range(2):
        sorted_cells[v] = place_acc[v * places : (v + 1) * places]
        first = (2 + 2 * v) * places
        sorted_cells[2 + v] = place_acc[first : first + places] + place_acc[first + places : first + 2 * places]

    def half_of(section):
        count = ring * cap_rows
        return sorted_cells.at[:, pl.ds(pl.multiple_of(section * count, 8), count), :]

    shared = to_partner(0, half_of(other), cells.at[sect])
    kept = pltpu.make_async_copy(half_of(sect), cells.at[sect], local_sem)
    shared.start()
    kept.start()

    @pl.when(lower)
    def _():
        handed.wait_recv()
        eliminate(hand[piece(tracers), :])
        ratios[levels - 1] = scale[...] * inverses[levels - 1]
        descend(lambda q: hand[piece(q), :], lambda q, carried: None)
        for q in range(tracers):
            low[piece(q), :] = parts[q, levels - 1]
        low[piece(tracers), :] = ratios[levels - 1]
        lowest.start()

    kept.wait()
    shared.wait()

    def arrange(i, _):
        here = pl.ds(pl.multiple_of(i * spot_rows, 8), spot_rows)

        def merged(v, k):
            piece = slice(k * cap_rows, (k + 1) * cap_rows)
            return jnp.concatenate([cells[0, v, here, :][piece], cells[1, v, here, :][piece]], axis=0)

        for k in range(2):
            col_row[2 * i + k] = merged(0, k).astype(jnp.int32)
            col_lane[2 * i + k] = merged(1, k).astype(jnp.int32)
            gain_sent[2 * i + k] = merged(2, k)
            flow[2 * i + k] = merged(3, k)
        return 0

    lax.fori_loop(0, ring // 2, arrange, 0)

    def send_gain(s, _):
        to(0, gain_sent, gain_came, s).start()
        return 0

    lax.fori_loop(1, ring, send_gain, 0)
    gain_came[me] = gain_sent[me]

    def send_all(step, g):
        here = slice(g * mine * rows, (g + 1) * mine * rows)
        bottom = low[here, :]
        if step:
            flux_over(step - 1, g).wait_recv()
            change = flux[step - 1, g] + flux_came[step - 1, g]
            bottom = bottom + jnp.concatenate([low[piece(tracers), :]] * mine, axis=0) * change
        table = table_of(bottom)

        def send(*steps):
            chips = [ahead(s) for s in steps]
            picked = [in_rows(p) for p in gather(table, line_of(col_row, chips), line_of(col_lane, chips), rows)]
            for j, (s, chip) in enumerate(zip(steps, chips)):
                sent[g, chip] = jnp.concatenate([p[j * spot_rows : (j + 1) * spot_rows] for p in picked], axis=0)
                if remote(s):
                    outward(step, g, s).start()

        in_fours(send)
        arrived[g, me] = sent[g, me]

    def tally():
        acc[...] = jnp.zeros_like(acc)

        def receive(*steps):
            chips = [behind(s) for s in steps]
            for s in steps:
                if remote(s):
                    to(0, gain_sent, gain_came, s).wait_recv()
            for chip in chips:
                here = pl.ds(pl.multiple_of(chip * spot_rows, 8), spot_rows)
                strength[chip] = gain_came[chip] * spots[2, here, :]
            force = jnp.concatenate([strength[chip] for chip in chips], axis=0)
            summed = scatter([force], spot(0, chips), spot(1, chips), surf_rows)
            acc[0:surf_rows] += summed[0:surf_rows] + summed[surf_rows:]

        in_fours(receive)
        inverse[...] = 1.0 / (1.0 + rate[...] * acc[0:surf_rows])

    def surface_all(step, g):
        acc[...] = jnp.zeros_like(acc)

        def receive(*steps):
            chips = [behind(s) for s in steps]
            for s in steps:
                if remote(s):
                    outward(step, g, s).wait_recv()
            values = [
                jnp.concatenate(
                    [arrived[g, chip, q * spot_rows : (q + 1) * spot_rows, :] * strength[chip] for chip in chips],
                    axis=0,
                )
                for q in range(mine)
            ]
            summed = scatter(values, spot(0, chips), spot(1, chips), surf_rows)
            acc[...] += summed[0 : mine * surf_rows] + summed[mine * surf_rows :]

        in_fours(receive)
        before = sea if step == 0 else sea_out
        for q in range(mine):
            here = slice(q * surf_rows, (q + 1) * surf_rows)
            there = slice((g * mine + q) * surf_rows, (g * mine + q + 1) * surf_rows)
            sea_out[there, :] = (before[there, :] + rate[...] * acc[here, :]) * inverse[...]
        table = table_of(sea_out[g * mine * surf_rows : (g + 1) * mine * surf_rows, :])

        def give_back(*steps):
            chips = [ahead(s) for s in steps]
            picked = [in_rows(p) for p in gather(table, spot(0, chips), spot(1, chips), surf_rows)]
            for j, (s, chip) in enumerate(zip(steps, chips)):
                back[g, chip] = jnp.concatenate([p[j * spot_rows : (j + 1) * spot_rows] for p in picked], axis=0)
                if remote(s):
                    homeward(step, g, s).start()

        in_fours(give_back)
        returned[g, me] = back[g, me]

    def take_all(step, g):
        flux[step, g] = jnp.zeros(flux.shape[2:], jnp.float32)

        def take_back(*steps):
            chips = [behind(s) for s in steps]
            for s in steps:
                if remote(s):
                    homeward(step, g, s).wait_recv()
            values = []
            for q in range(mine):
                here = slice(q * spot_rows, (q + 1) * spot_rows)
                values.append(
                    jnp.concatenate(
                        [(returned[g, chip, here, :] - sent[g, chip, here, :]) * flow[chip] for chip in chips], axis=0
                    )
                )
            summed = scatter(values, line_of(col_row, chips), line_of(col_lane, chips), rows)
            flux[step, g] += summed[0 : mine * rows] + summed[mine * rows :]

        in_fours(take_back)
        flux_over(step, g).start()

        def finish(s, _):
            outward(step, g, s).wait_send()
            homeward(step, g, s).wait_send()
            return 0

        lax.fori_loop(1, ring, finish, 0)

    @pl.when(upper)
    def _():
        handed.wait_send()
        lowest.wait_recv()

    for g in range(GROUPS):
        send_all(0, g)
    tally()

    @pl.when(lower)
    def _():
        for q in range(0, tracers, 2):

            def rise(i, values):
                k = levels - 2 - i
                return [parts[q + j, k] + ratios[k] * value for j, value in enumerate(values)]

            values = lax.fori_loop(0, levels - 1, rise, [parts[q + j, levels - 1] for j in range(2)], unroll=4)
            for j in range(2):
                top[piece(q + j), :] = values[j]
        top[piece(tracers), :] = lax.fori_loop(
            0, levels - 1, lambda i, value: value * ratios[levels - 2 - i], ratios[levels - 1], unroll=4
        )
        highest.start()

    for step in range(SUBSTEPS):
        for g in range(GROUPS):
            surface_all(step, g)
        for g in range(GROUPS):
            take_all(step, g)
        if step < SUBSTEPS - 1:
            for g in range(GROUPS):
                send_all(step + 1, g)

    def finish(s, _):
        to(0, gain_sent, gain_came, s).wait_send()
        return 0

    lax.fori_loop(1, ring, finish, 0)

    @pl.when(lower)
    def _():
        lowest.wait_send()
        highest.wait_send()

    @pl.when(upper)
    def _():
        highest.wait_recv()

    for g in range(GROUPS):
        here = slice(g * mine * rows, (g + 1) * mine * rows)
        flux_over(SUBSTEPS - 1, g).wait_recv()
        below[here, :] = flux[SUBSTEPS - 1, g] + flux_came[SUBSTEPS - 1, g]

    @pl.when(upper)
    def _():
        for q in range(tracers):
            below[piece(q), :] = top[piece(q), :] + top[piece(tracers), :] * below[piece(q), :]

    for step in range(SUBSTEPS):
        for g in range(GROUPS):
            flux_over(step, g).wait_send()


def forward(air, mix, scale, owner, column, coef, weight, counts, spots, sea, rate, ring, cap_rows):
    tracers, levels, _ = air.shape
    rows, surf_rows = scale.shape[0], rate.shape[0]
    mine = tracers // GROUPS
    places = 2 * ring * cap_rows
    step_rows = max(2, min(16, 2048 // places))
    while owner.shape[0] % step_rows:
        step_rows -= 2

    def real(*shape):
        return pltpu.VMEM(shape, jnp.float32)

    message = real(GROUPS, ring, mine * 2 * cap_rows, LANES)
    once = real(ring, 2 * cap_rows, LANES)
    column_state = real((tracers + 1) * rows, LANES)
    phases = 1 + 2 * SUBSTEPS * GROUPS
    return pl.pallas_call(
        functools.partial(forward_kernel, tracers, ring, cap_rows, step_rows),
        out_shape=[
            jax.ShapeDtypeStruct((tracers, levels, rows, LANES), jnp.float32),
            jax.ShapeDtypeStruct((levels, rows, LANES), jnp.float32),
            jax.ShapeDtypeStruct((tracers * rows, LANES), jnp.float32),
            jax.ShapeDtypeStruct(sea.shape, jnp.float32),
        ],
        in_specs=[HBM] * 2 + [VMEM] * 9,
        out_specs=[VMEM] * 4,
        scratch_shapes=[
            real(levels, rows, LANES),
            real(levels, rows, LANES),
            column_state,
            column_state,
            column_state,
            real(6 * places, LANES),
            real(2 * ring, LANES),
            real(4, places, LANES),
            real(2, 4, ring * cap_rows, LANES),
            pltpu.VMEM((ring, 2 * cap_rows, LANES), jnp.int32),
            pltpu.VMEM((ring, 2 * cap_rows, LANES), jnp.int32),
            once,
            once,
            once,
            once,
            real(surf_rows, LANES),
            message,
            message,
            message,
            message,
            real(SUBSTEPS, GROUPS, mine * rows, LANES),
            real(SUBSTEPS, GROUPS, mine * rows, LANES),
            real(mine * surf_rows, LANES),
            pltpu.SemaphoreType.DMA((phases, ring)),
            pltpu.SemaphoreType.DMA((phases, ring)),
            pltpu.SemaphoreType.DMA((4 + SUBSTEPS * GROUPS,)),
            pltpu.SemaphoreType.DMA((4 + SUBSTEPS * GROUPS,)),
            pltpu.SemaphoreType.DMA,
            pltpu.SemaphoreType.DMA((2, rows)),
        ],
        compiler_params=pltpu.CompilerParams(
            vmem_limit_bytes=40 * 1024 * 1024, collective_id=0, has_side_effects=True
        ),
    )(air, mix, scale, owner, column, coef, weight, counts, spots, sea, rate)


def ascend_kernel(parts, ratios, below, out, risen, sem):
    tracers, levels, rows, _ = parts.shape
    tile = 8

    def store(j):
        here = pl.ds(pl.multiple_of(j * LANES, LANES), LANES)
        return pltpu.make_async_copy(risen.at[:, :, j, :], out.at[:, :, here], sem.at[j])

    def columns(i, _):
        here = pl.ds(pl.multiple_of(i * tile, tile), tile)

        def level(n, values):
            k = levels - 1 - n
            ratio = ratios[k, here, :]
            values = [parts[q, k, here, :] + ratio * value for q, value in enumerate(values)]
            for q, value in enumerate(values):
                risen[q, k, here, :] = value
            return values

        start = [below[pl.ds(pl.multiple_of(q * rows + i * tile, tile), tile), :] for q in range(tracers)]
        lax.fori_loop(0, levels, level, start, unroll=8)

        def send(j, _):
            store(i * tile + j).start()
            return 0

        lax.fori_loop(0, tile, send, 0)
        return 0

    lax.fori_loop(0, rows // tile, columns, 0)

    def finish(j, _):
        store(j).wait()
        return 0

    lax.fori_loop(0, rows, finish, 0)


def ascend(parts, ratios, below):
    tracers, levels, rows, _ = parts.shape
    return pl.pallas_call(
        ascend_kernel,
        in_specs=[VMEM] * 3,
        out_specs=HBM,
        out_shape=jax.ShapeDtypeStruct((tracers, levels, rows * LANES), jnp.float32),
        scratch_shapes=[pltpu.VMEM(parts.shape, jnp.float32), pltpu.SemaphoreType.DMA((rows,))],
        compiler_params=pltpu.CompilerParams(vmem_limit_bytes=16 * 1024 * 1024),
    )(parts, ratios, below)


def body(
    air_state,
    mix_coef,
    flux_scale,
    sea_state,
    sea_rate,
    block_counts,
    cell_column,
    cell_owner,
    cell_coef,
    cell_weight,
    slot_cell,
    slot_frac,
):
    tracers, columns = air_state.shape[1:]
    ring = lax.axis_size("cols")
    rows = columns // BLOCK_COLS
    surf_cells = sea_state.shape[1]
    surf_rows = surf_cells // LANES
    capacity = slot_cell.shape[0] // (2 * ring)
    cap_rows = max(4, -(-capacity // LANES))

    def by_chip(values):
        values = jnp.pad(values.reshape(2, ring, capacity), ((0, 0), (0, 0), (0, cap_rows * LANES - capacity)))
        values = jnp.swapaxes(values.reshape(2, ring, cap_rows, LANES), 0, 1)
        return values.reshape(ring * 2 * cap_rows, LANES)

    cell = by_chip(slot_cell)
    spots = jnp.stack([(cell // LANES).astype(jnp.float32), (cell % LANES).astype(jnp.float32), by_chip(slot_frac)])
    parts, ratios, below, sea = forward(
        jnp.swapaxes(air_state, 0, 1),
        mix_coef,
        flux_scale.reshape(rows, LANES),
        cell_owner.reshape(-1, LANES),
        cell_column.reshape(-1, LANES),
        cell_coef.reshape(-1, LANES),
        cell_weight.reshape(-1, LANES),
        jnp.broadcast_to(block_counts.reshape(-1, 1, 1), (rows, 2, LANES)).reshape(-1, LANES),
        spots,
        sea_state.reshape(tracers * surf_rows, LANES),
        sea_rate.reshape(surf_rows, LANES),
        ring,
        cap_rows,
    )
    return (jnp.swapaxes(ascend(parts, ratios, below), 0, 1), sea.reshape(tracers, surf_cells))


def solution(mesh):
    return jax.shard_map(
        body,
        mesh=mesh,
        in_specs=(
            P("sect", None, "cols"),
            P("sect", "cols"),
            P("cols"),
            P(None, ("sect", "cols")),
            P(("sect", "cols")),
            P(("sect", "cols"), None),
            P(("sect", "cols")),
            P(("sect", "cols"), None),
            P(("sect", "cols")),
            P(("sect", "cols")),
            P(("sect", "cols")),
            P(("sect", "cols")),
        ),
        out_specs=(P("sect", None, "cols"), P(None, ("sect", "cols"))),
        check_vma=False,
    )
```

```python
import functools
import math

import jax
import jax.numpy as jnp
from jax import lax
from jax.experimental import pallas as pl
from jax.experimental.pallas import tpu as pltpu
from jax.sharding import PartitionSpec as P

BLOCK_COLS = 128
BLOCK_SLOTS = 256
SUBSTEPS = 2
GROUPS = 2
LANES = 128
LIMIT = 56 * 1024 * 1024
HBM = pl.BlockSpec(memory_space=pltpu.HBM)


def split(value):
    high = value.astype(jnp.bfloat16).astype(jnp.float32)
    return high, value - high


def hot(index, count):
    places = lax.broadcasted_iota(jnp.int32, (count, index.shape[1]), 0).astype(jnp.int16)
    return jnp.where(places == index.astype(jnp.int16), jnp.ones((), jnp.bfloat16), jnp.zeros((), jnp.bfloat16))


def in_line(packed):
    return jnp.concatenate([packed[r : r + 1] for r in range(packed.shape[0])], axis=1)


def in_rows(line):
    return jnp.concatenate([line[:, r : r + LANES] for r in range(0, line.shape[1], LANES)], axis=0)


def scatter(values, row, lane, rows):
    mask = hot(row, rows)
    parts = [split(value) for value in values]
    lines = [in_line(p[0]) for p in parts] + [in_line(p[1]) for p in parts]
    return lax.dot_general(
        jnp.concatenate([mask * line.astype(jnp.bfloat16) for line in lines], axis=0),
        hot(lane, LANES),
        (((1,), (1,)), ((), ())),
        preferred_element_type=jnp.float32,
    )


def table_of(value):
    high, low = split(value)
    return jnp.concatenate([high, low], axis=1).astype(jnp.bfloat16)


def gather(table, row, lane, rows):
    lane_hot = hot(lane, LANES)
    picked = jnp.dot(table, jnp.concatenate([lane_hot, lane_hot], axis=0), preferred_element_type=jnp.float32)
    mask = lax.broadcasted_iota(jnp.int32, (rows, row.shape[1]), 0) == row
    return [
        jnp.sum(jnp.where(mask, picked[q : q + rows], 0.0), axis=0, keepdims=True)
        for q in range(0, table.shape[0], rows)
    ]


def forward_kernel(
    tracers,
    ring,
    cap_rows,
    step_rows,
    capacity,
    air,
    mix,
    scale_in,
    sea_in,
    rate_in,
    counts_in,
    column_in,
    owner_in,
    coef_in,
    weight_in,
    cell_in,
    frac_in,
    parts_out,
    ratios_out,
    below_out,
    sea_new,
    parts,
    ratios,
    below,
    sea_out,
    scale,
    sea,
    rate,
    counts,
    column,
    owner,
    coef,
    weight,
    slot_cell,
    slot_frac,
    spots,
    mixes,
    inverses,
    hand,
    low,
    top,
    place_acc,
    offset,
    sorted_cells,
    cells,
    col_row,
    col_lane,
    flow,
    gain_sent,
    gain_came,
    strength,
    inverse,
    sent,
    arrived,
    back,
    returned,
    flux,
    flux_came,
    acc,
    send_sem,
    recv_sem,
    pair_send,
    pair_recv,
    local_sem,
    load_sem,
    fetch_sem,
    store_sem,
):
    levels, rows = ratios.shape[0], ratios.shape[1]
    surf_rows = rate.shape[0]
    devices = 2 * ring
    mine = tracers // GROUPS
    spot_rows = 2 * cap_rows
    sect = lax.axis_index("sect")
    me = lax.axis_index("cols")
    other = 1 - sect

    def ahead(s):
        return lax.rem(me + s, ring)

    def behind(s):
        return lax.rem(me + ring - s, ring)

    def remote(s):
        return not (isinstance(s, int) and s == 0)

    def to(phase, source, target, s):
        return pltpu.make_async_remote_copy(
            src_ref=source.at[ahead(s)],
            dst_ref=target.at[me],
            send_sem=send_sem.at[phase, s],
            recv_sem=recv_sem.at[phase, s],
            device_id=(sect, ahead(s)),
            device_id_type=pl.DeviceIdType.MESH,
        )

    def outward(step, g, s):
        return to(1 + 2 * (step * GROUPS + g), sent.at[g], arrived.at[g], s)

    def homeward(step, g, s):
        return to(2 + 2 * (step * GROUPS + g), back.at[g], returned.at[g], s)

    def to_partner(k, source, target):
        return pltpu.make_async_remote_copy(
            src_ref=source,
            dst_ref=target,
            send_sem=pair_send.at[k],
            recv_sem=pair_recv.at[k],
            device_id=(other, me),
            device_id_type=pl.DeviceIdType.MESH,
        )

    def flux_over(step, g):
        return to_partner(1 + step * GROUPS + g, flux.at[step, g], flux_came.at[step, g])

    def in_fours(act):
        def far(i, _):
            act(*[ring // 2 + 4 * i + j for j in range(4)])
            return 0

        def near(i, _):
            act(*[ring // 2 - 1 - 4 * i - j for j in range(4)])
            return 0

        lax.fori_loop(0, ring // 8, far, 0)
        lax.fori_loop(0, ring // 8 - 1, near, 0)
        act(3, 2, 1, 0)

    def line_of(ref, chips):
        return in_line(jnp.concatenate([ref[chip] for chip in chips], axis=0))

    def spot(v, chips):
        return in_line(
            jnp.concatenate(
                [spots[v, pl.ds(pl.multiple_of(chip * spot_rows, 8), spot_rows), :] for chip in chips], axis=0
            )
        ).astype(jnp.int32)

    barrier = pltpu.get_barrier_semaphore()

    def greet(s, _):
        pl.semaphore_signal(barrier, inc=1, device_id=(sect, ahead(s)), device_id_type=pl.DeviceIdType.MESH)
        return 0

    lax.fori_loop(1, ring, greet, 0)
    pl.semaphore_signal(barrier, inc=1, device_id=(other, me), device_id_type=pl.DeviceIdType.MESH)

    def load(j):
        here = pl.ds(pl.multiple_of(j * LANES, LANES), LANES)
        return [
            pltpu.make_async_copy(mix.at[:, here], mixes.at[:, j, :], load_sem.at[0, j]),
            pltpu.make_async_copy(air.at[:, :, here], parts.at[:, :, j, :], load_sem.at[1, j]),
        ]

    def start_load(j, _):
        for copy in load(j):
            copy.start()
        return 0

    def wait_load(j, _):
        for copy in load(j):
            copy.wait()
        return 0

    slot_rows = cell_in.shape[0]
    first_fetches = [(counts_in, counts), (owner_in, owner), (column_in, column), (coef_in, coef), (weight_in, weight)]
    later_fetches = [
        (scale_in, scale),
        (rate_in, rate),
        (cell_in, slot_cell.at[pl.ds(0, slot_rows)]),
        (frac_in, slot_frac.at[pl.ds(0, slot_rows)]),
    ]
    fetches = [
        pltpu.make_async_copy(source, target, fetch_sem.at[i])
        for i, (source, target) in enumerate(first_fetches + later_fetches)
    ]
    first_fetches, later_fetches = fetches[: len(first_fetches)], fetches[len(first_fetches) :]
    for copy in first_fetches:
        copy.start()
    lax.fori_loop(0, rows, start_load, 0)
    for copy in later_fetches:
        copy.start()

    def sea_part(j):
        here = pl.ds(pl.multiple_of(j * LANES, LANES), LANES)
        return pltpu.make_async_copy(sea_in.at[:, here], sea.at[:, j, :], load_sem.at[2, j])

    def start_sea(j, _):
        sea_part(j).start()
        return 0

    def wait_sea(j, _):
        sea_part(j).wait()
        return 0

    lax.fori_loop(0, surf_rows, start_sea, 0)
    for copy in first_fetches:
        copy.wait()
    block_of = lax.broadcasted_iota(jnp.int32, (owner.shape[0], counts.shape[1]), 0) // 2
    chosen = lax.broadcasted_iota(jnp.int32, (owner.shape[0], counts.shape[1]), 1) == block_of
    live = jnp.sum(jnp.where(chosen, counts[...].astype(jnp.float32), 0.0), axis=1, keepdims=True)
    places_in = lax.broadcasted_iota(jnp.int32, owner.shape, 1) + LANES * lax.rem(
        lax.broadcasted_iota(jnp.int32, owner.shape, 0), 2
    )
    coef[...] = jnp.where(places_in.astype(jnp.float32) < live, coef[...], 0.0)

    places = devices * cap_rows
    blocks = step_rows * LANES // BLOCK_SLOTS
    place_acc[...] = jnp.zeros_like(place_acc)
    offset[...] = jnp.zeros_like(offset)
    later = (
        lax.broadcasted_iota(jnp.int32, (BLOCK_SLOTS, BLOCK_SLOTS), 0)
        <= lax.broadcasted_iota(jnp.int32, (BLOCK_SLOTS, BLOCK_SLOTS), 1)
    )
    later = jnp.where(later, 1.0, 0.0).astype(jnp.bfloat16)
    numbers = lax.broadcasted_iota(jnp.int32, (step_rows, LANES), 0)

    def sort_part(i, _):
        here = pl.ds(pl.multiple_of(i * step_rows, step_rows), step_rows)
        own = in_line(owner[here, :])
        named = hot(own, devices)
        named_blocks = [named[:, b * BLOCK_SLOTS : (b + 1) * BLOCK_SLOTS] for b in range(blocks)]
        running = jnp.dot(jnp.concatenate(named_blocks, axis=0), later, preferred_element_type=jnp.float32)
        before = offset[...]
        ranks = []
        for b in range(blocks):
            wide = named_blocks[b].astype(jnp.float32)
            count = running[b * devices : (b + 1) * devices] + before[:, 0:1]
            ranks.append(jnp.sum(wide * count, axis=0, keepdims=True) - 1.0)
            before = before + jnp.broadcast_to(jnp.sum(wide, axis=1, keepdims=True), before.shape)
        offset[...] = before
        rank = jnp.concatenate(ranks, axis=1).astype(jnp.int32)
        gain = coef[here, :]
        gain_high, gain_low = split(gain)
        flow_high, flow_low = split(weight[here, :] * gain)
        values = [
            ((i * step_rows + numbers) // 2).astype(jnp.float32),
            column[here, :].astype(jnp.float32),
            gain_high,
            gain_low,
            flow_high,
            flow_low,
        ]
        mask = hot(own * cap_rows + rank // LANES, places)
        place_acc[...] += lax.dot_general(
            jnp.concatenate([mask * in_line(value).astype(jnp.bfloat16) for value in values], axis=0),
            hot(lax.rem(rank, LANES), LANES),
            (((1,), (1,)), ((), ())),
            preferred_element_type=jnp.float32,
        )
        return 0

    def eliminate(under):
        def coefficients(k, under):
            coupling = mixes[k]
            inv = 1.0 / (1.0 + coupling + under)
            ratio = coupling * inv
            inverses[k] = inv
            ratios[k] = ratio
            return ratio * (1.0 + under)

        return lax.fori_loop(0, levels, coefficients, under, unroll=4)

    def descend(carried_of, keep):
        for q in range(0, tracers, 2):

            def level(k, carried):
                ratio, inv = ratios[k], inverses[k]
                result = []
                for j, value in enumerate(carried):
                    value = parts[q + j, k] + value
                    parts[q + j, k] = value * inv
                    result.append(value * ratio)
                return result

            keep(q, lax.fori_loop(0, levels, level, [carried_of(q), carried_of(q + 1)], unroll=4))

    handed = to_partner(1 + SUBSTEPS * GROUPS, hand, hand)
    lowest = to_partner(2 + SUBSTEPS * GROUPS, low, low)
    highest = to_partner(3 + SUBSTEPS * GROUPS, top, top)
    upper, lower = sect == 0, sect == 1

    def piece(q):
        return slice(q * rows, (q + 1) * rows)

    sort_steps = owner.shape[0] // step_rows
    early = sort_steps // 3
    lax.fori_loop(0, early, sort_part, 0)
    pl.semaphore_wait(barrier, ring)
    lax.fori_loop(0, rows, wait_load, 0)
    later_fetches[0].wait()

    @pl.when(upper)
    def _():
        zero = jnp.zeros((rows, LANES), jnp.float32)
        hand[piece(tracers), :] = eliminate(zero)

        def keep(q, carried):
            hand[piece(q), :] = carried[0]
            hand[piece(q + 1), :] = carried[1]

        descend(lambda q: zero, keep)
        handed.start()

    lax.fori_loop(early, sort_steps, sort_part, 0)
    for v in range(2):
        sorted_cells[v] = place_acc[v * places : (v + 1) * places]
        first = (2 + 2 * v) * places
        sorted_cells[2 + v] = place_acc[first : first + places] + place_acc[first + places : first + 2 * places]

    def half_of(section):
        count = ring * cap_rows
        return sorted_cells.at[:, pl.ds(pl.multiple_of(section * count, 8), count), :]

    shared = to_partner(0, half_of(other), cells.at[sect])
    kept = pltpu.make_async_copy(half_of(sect), cells.at[sect], local_sem)
    shared.start()
    kept.start()

    @pl.when(lower)
    def _():
        handed.wait_recv()
        eliminate(hand[piece(tracers), :])
        ratios[levels - 1] = scale[...] * inverses[levels - 1]
        descend(lambda q: hand[piece(q), :], lambda q, carried: None)
        for q in range(tracers):
            low[piece(q), :] = parts[q, levels - 1]
        low[piece(tracers), :] = ratios[levels - 1]
        lowest.start()

    stores = [
        pltpu.make_async_copy(source, target, store_sem.at[i])
        for i, (source, target) in enumerate(
            [(parts, parts_out), (ratios, ratios_out), (sea_out, sea_new), (below, below_out)]
        )
    ]
    stores[0].start()
    stores[1].start()
    for copy in later_fetches[2:]:
        copy.wait()
    beyond = pl.ds(slot_rows, slot_cell.shape[0] - slot_rows)
    slot_cell[beyond, :] = jnp.zeros((slot_cell.shape[0] - slot_rows, LANES), jnp.int32)
    slot_frac[beyond, :] = jnp.zeros((slot_cell.shape[0] - slot_rows, LANES), jnp.float32)
    period = LANES // math.gcd(capacity, LANES)
    lane_numbers = lax.broadcasted_iota(jnp.int32, (cap_rows, LANES), 1)

    def cut(ref, row, shift):
        window = jnp.concatenate([ref[pl.ds(row + r, 1), :] for r in range(cap_rows + 1)], axis=0)
        if shift == 0:
            return window[:cap_rows]
        turned = pltpu.roll(window, LANES - shift, 1)
        return jnp.where(lane_numbers < LANES - shift, turned[:cap_rows], turned[1:])

    def place_spots(i, _):
        for j in range(period):
            source = i * period + j
            row = i * (period * capacity // LANES) + j * capacity // LANES
            cell = cut(slot_cell, row, j * capacity % LANES)
            frac = cut(slot_frac, row, j * capacity % LANES)
            start = lax.rem(source, ring) * spot_rows + source // ring * cap_rows
            for r in range(cap_rows):
                line = pl.ds(start + r, 1)
                spots[0, line, :] = (cell[r : r + 1] // LANES).astype(jnp.float32)
                spots[1, line, :] = lax.rem(cell[r : r + 1], LANES).astype(jnp.float32)
                spots[2, line, :] = frac[r : r + 1]
        return 0

    lax.fori_loop(0, devices // period, place_spots, 0)
    later_fetches[1].wait()
    lax.fori_loop(0, surf_rows, wait_sea, 0)
    kept.wait()
    shared.wait()

    def arrange(i, _):
        here = pl.ds(pl.multiple_of(i * spot_rows, 8), spot_rows)

        def merged(v, k):
            piece = slice(k * cap_rows, (k + 1) * cap_rows)
            return jnp.concatenate([cells[0, v, here, :][piece], cells[1, v, here, :][piece]], axis=0)

        for k in range(2):
            col_row[2 * i + k] = merged(0, k).astype(jnp.int32)
            col_lane[2 * i + k] = merged(1, k).astype(jnp.int32)
            gain_sent[2 * i + k] = merged(2, k)
            flow[2 * i + k] = merged(3, k)
        return 0

    lax.fori_loop(0, ring // 2, arrange, 0)

    def send_gain(s, _):
        to(0, gain_sent, gain_came, s).start()
        return 0

    lax.fori_loop(1, ring, send_gain, 0)
    gain_came[me] = gain_sent[me]

    def send_all(step, g):
        here = slice(g * mine * rows, (g + 1) * mine * rows)
        bottom = low[here, :]
        if step:
            flux_over(step - 1, g).wait_recv()
            change = flux[step - 1, g] + flux_came[step - 1, g]
            bottom = bottom + jnp.concatenate([low[piece(tracers), :]] * mine, axis=0) * change
        table = table_of(bottom)

        def send(*steps):
            chips = [ahead(s) for s in steps]
            picked = [in_rows(p) for p in gather(table, line_of(col_row, chips), line_of(col_lane, chips), rows)]
            for j, (s, chip) in enumerate(zip(steps, chips)):
                sent[g, chip] = jnp.concatenate([p[j * spot_rows : (j + 1) * spot_rows] for p in picked], axis=0)
                if remote(s):
                    outward(step, g, s).start()

        in_fours(send)
        arrived[g, me] = sent[g, me]

    def tally():
        acc[...] = jnp.zeros_like(acc)

        def receive(*steps):
            chips = [behind(s) for s in steps]
            for s in steps:
                if remote(s):
                    to(0, gain_sent, gain_came, s).wait_recv()
            for chip in chips:
                here = pl.ds(pl.multiple_of(chip * spot_rows, 8), spot_rows)
                strength[chip] = gain_came[chip] * spots[2, here, :]
            force = jnp.concatenate([strength[chip] for chip in chips], axis=0)
            summed = scatter([force], spot(0, chips), spot(1, chips), surf_rows)
            acc[0:surf_rows] += summed[0:surf_rows] + summed[surf_rows:]

        in_fours(receive)
        inverse[...] = 1.0 / (1.0 + rate[...] * acc[0:surf_rows])

    def surface_all(step, g):
        acc[...] = jnp.zeros_like(acc)

        def receive(*steps):
            chips = [behind(s) for s in steps]
            for s in steps:
                if remote(s):
                    outward(step, g, s).wait_recv()
            values = [
                jnp.concatenate(
                    [arrived[g, chip, q * spot_rows : (q + 1) * spot_rows, :] * strength[chip] for chip in chips],
                    axis=0,
                )
                for q in range(mine)
            ]
            summed = scatter(values, spot(0, chips), spot(1, chips), surf_rows)
            acc[...] += summed[0 : mine * surf_rows] + summed[mine * surf_rows :]

        in_fours(receive)
        for q in range(mine):
            here = slice(q * surf_rows, (q + 1) * surf_rows)
            there = slice((g * mine + q) * surf_rows, (g * mine + q + 1) * surf_rows)
            before = sea[g * mine + q] if step == 0 else sea_out[there, :]
            sea_out[there, :] = (before + rate[...] * acc[here, :]) * inverse[...]
        table = table_of(sea_out[g * mine * surf_rows : (g + 1) * mine * surf_rows, :])

        def give_back(*steps):
            chips = [ahead(s) for s in steps]
            picked = [in_rows(p) for p in gather(table, spot(0, chips), spot(1, chips), surf_rows)]
            for j, (s, chip) in enumerate(zip(steps, chips)):
                back[g, chip] = jnp.concatenate([p[j * spot_rows : (j + 1) * spot_rows] for p in picked], axis=0)
                if remote(s):
                    homeward(step, g, s).start()

        in_fours(give_back)
        returned[g, me] = back[g, me]

    def take_all(step, g):
        flux[step, g] = jnp.zeros(flux.shape[2:], jnp.float32)

        def take_back(*steps):
            chips = [behind(s) for s in steps]
            for s in steps:
                if remote(s):
                    homeward(step, g, s).wait_recv()
            values = []
            for q in range(mine):
                here = slice(q * spot_rows, (q + 1) * spot_rows)
                values.append(
                    jnp.concatenate(
                        [(returned[g, chip, here, :] - sent[g, chip, here, :]) * flow[chip] for chip in chips], axis=0
                    )
                )
            summed = scatter(values, line_of(col_row, chips), line_of(col_lane, chips), rows)
            flux[step, g] += summed[0 : mine * rows] + summed[mine * rows :]

        in_fours(take_back)
        flux_over(step, g).start()

        def finish(s, _):
            outward(step, g, s).wait_send()
            homeward(step, g, s).wait_send()
            return 0

        lax.fori_loop(1, ring, finish, 0)

    @pl.when(upper)
    def _():
        handed.wait_send()
        lowest.wait_recv()

    for g in range(GROUPS):
        send_all(0, g)
    tally()

    @pl.when(lower)
    def _():
        for q in range(0, tracers, 2):

            def rise(i, values):
                k = levels - 2 - i
                return [parts[q + j, k] + ratios[k] * value for j, value in enumerate(values)]

            values = lax.fori_loop(0, levels - 1, rise, [parts[q + j, levels - 1] for j in range(2)], unroll=4)
            for j in range(2):
                top[piece(q + j), :] = values[j]
        top[piece(tracers), :] = lax.fori_loop(
            0, levels - 1, lambda i, value: value * ratios[levels - 2 - i], ratios[levels - 1], unroll=4
        )
        highest.start()

    for step in range(SUBSTEPS):
        for g in range(GROUPS):
            surface_all(step, g)
        for g in range(GROUPS):
            take_all(step, g)
        if step < SUBSTEPS - 1:
            for g in range(GROUPS):
                send_all(step + 1, g)

    stores[2].start()

    def finish(s, _):
        to(0, gain_sent, gain_came, s).wait_send()
        return 0

    lax.fori_loop(1, ring, finish, 0)

    @pl.when(lower)
    def _():
        lowest.wait_send()
        highest.wait_send()

    @pl.when(upper)
    def _():
        highest.wait_recv()

    for g in range(GROUPS):
        here = slice(g * mine * rows, (g + 1) * mine * rows)
        flux_over(SUBSTEPS - 1, g).wait_recv()
        below[here, :] = flux[SUBSTEPS - 1, g] + flux_came[SUBSTEPS - 1, g]

    @pl.when(upper)
    def _():
        for q in range(tracers):
            below[piece(q), :] = top[piece(q), :] + top[piece(tracers), :] * below[piece(q), :]

    stores[3].start()

    for step in range(SUBSTEPS):
        for g in range(GROUPS):
            flux_over(step, g).wait_send()
    for copy in stores:
        copy.wait()


def forward(air, mix, scale, sea, rate, counts, column, owner, coef, weight, cell, frac, ring, cap_rows, capacity):
    tracers, levels, _ = air.shape
    rows, surf_rows = scale.shape[0], rate.shape[0]
    mine = tracers // GROUPS
    places = 2 * ring * cap_rows
    step_rows = max(2, min(16, 2048 // places))
    while owner.shape[0] % step_rows:
        step_rows -= 2

    def real(*shape):
        return pltpu.VMEM(shape, jnp.float32)

    message = real(GROUPS, ring, mine * 2 * cap_rows, LANES)
    once = real(ring, 2 * cap_rows, LANES)
    column_state = real((tracers + 1) * rows, LANES)
    phases = 1 + 2 * SUBSTEPS * GROUPS
    return pl.pallas_call(
        functools.partial(forward_kernel, tracers, ring, cap_rows, step_rows, capacity),
        out_shape=[
            jax.ShapeDtypeStruct((tracers, levels, rows, LANES), jnp.float32),
            jax.ShapeDtypeStruct((levels, rows, LANES), jnp.float32),
            jax.ShapeDtypeStruct((tracers * rows, LANES), jnp.float32),
            jax.ShapeDtypeStruct((tracers * surf_rows, LANES), jnp.float32),
        ],
        in_specs=[HBM] * 12,
        out_specs=[HBM] * 4,
        scratch_shapes=[
            real(tracers, levels, rows, LANES),
            real(levels, rows, LANES),
            real(tracers * rows, LANES),
            real(tracers * surf_rows, LANES),
            real(rows, LANES),
            real(tracers, surf_rows, LANES),
            real(surf_rows, LANES),
            pltpu.VMEM(counts.shape, jnp.int32),
            pltpu.VMEM(column.shape, jnp.int32),
            pltpu.VMEM(owner.shape, jnp.int32),
            real(*coef.shape),
            real(*weight.shape),
            pltpu.VMEM((cell.shape[0] + 8, LANES), jnp.int32),
            real(frac.shape[0] + 8, LANES),
            real(3, ring * 2 * cap_rows, LANES),
            real(levels, rows, LANES),
            real(levels, rows, LANES),
            column_state,
            column_state,
            column_state,
            real(6 * places, LANES),
            real(2 * ring, LANES),
            real(4, places, LANES),
            real(2, 4, ring * cap_rows, LANES),
            pltpu.VMEM((ring, 2 * cap_rows, LANES), jnp.int32),
            pltpu.VMEM((ring, 2 * cap_rows, LANES), jnp.int32),
            once,
            once,
            once,
            once,
            real(surf_rows, LANES),
            message,
            message,
            message,
            message,
            real(SUBSTEPS, GROUPS, mine * rows, LANES),
            real(SUBSTEPS, GROUPS, mine * rows, LANES),
            real(mine * surf_rows, LANES),
            pltpu.SemaphoreType.DMA((phases, ring)),
            pltpu.SemaphoreType.DMA((phases, ring)),
            pltpu.SemaphoreType.DMA((4 + SUBSTEPS * GROUPS,)),
            pltpu.SemaphoreType.DMA((4 + SUBSTEPS * GROUPS,)),
            pltpu.SemaphoreType.DMA,
            pltpu.SemaphoreType.DMA((3, rows)),
            pltpu.SemaphoreType.DMA((9,)),
            pltpu.SemaphoreType.DMA((4,)),
        ],
        compiler_params=pltpu.CompilerParams(
            vmem_limit_bytes=LIMIT, collective_id=0, has_side_effects=True
        ),
    )(air, mix, scale, sea, rate, counts, column, owner, coef, weight, cell, frac)


def ascend_kernel(parts_in, ratios_in, below_in, sea, out, sea_out, risen, ratios, below, load_sem, sem, sea_sem):
    tracers, levels, rows, _ = risen.shape
    tile = 8
    tiles = rows // tile

    def store_sea(j):
        here = pl.ds(pl.multiple_of(j * LANES, LANES), LANES)
        return pltpu.make_async_copy(sea.at[:, j, :], sea_out.at[:, here], sea_sem.at[j])

    def start_sea(j, _):
        store_sea(j).start()
        return 0

    def finish_sea(j, _):
        store_sea(j).wait()
        return 0

    def load(i):
        here = pl.ds(pl.multiple_of(i * tile, tile), tile)
        return pltpu.make_async_copy(parts_in.at[:, :, here, :], risen.at[:, :, here, :], load_sem.at[i])

    def store(j):
        here = pl.ds(pl.multiple_of(j * LANES, LANES), LANES)
        return pltpu.make_async_copy(risen.at[:, :, j, :], out.at[:, :, here], sem.at[j])

    firsts = [
        pltpu.make_async_copy(ratios_in, ratios, load_sem.at[tiles]),
        pltpu.make_async_copy(below_in, below, load_sem.at[tiles + 1]),
    ]
    load(0).start()
    for copy in firsts:
        copy.start()
    for i in range(1, tiles):
        load(i).start()
    lax.fori_loop(0, sea.shape[1], start_sea, 0)
    for copy in firsts:
        copy.wait()

    def columns(i, _):
        here = pl.ds(pl.multiple_of(i * tile, tile), tile)
        load(i).wait()

        def level(n, values):
            k = levels - 1 - n
            ratio = ratios[k, here, :]
            values = [risen[q, k, here, :] + ratio * value for q, value in enumerate(values)]
            for q, value in enumerate(values):
                risen[q, k, here, :] = value
            return values

        start = [below[pl.ds(pl.multiple_of(q * rows + i * tile, tile), tile), :] for q in range(tracers)]
        lax.fori_loop(0, levels, level, start, unroll=8)

        def send(j, _):
            store(i * tile + j).start()
            return 0

        lax.fori_loop(0, tile, send, 0)
        return 0

    lax.fori_loop(0, tiles, columns, 0)

    def finish(j, _):
        store(j).wait()
        return 0

    lax.fori_loop(0, rows, finish, 0)
    lax.fori_loop(0, sea.shape[1], finish_sea, 0)


def ascend(parts, ratios, below, sea):
    tracers, levels, rows, _ = parts.shape
    return pl.pallas_call(
        ascend_kernel,
        in_specs=[HBM] * 4,
        out_specs=[HBM] * 2,
        out_shape=[
            jax.ShapeDtypeStruct((tracers, levels, rows * LANES), jnp.float32),
            jax.ShapeDtypeStruct((tracers, sea.shape[1] * LANES), jnp.float32),
        ],
        scratch_shapes=[
            pltpu.VMEM(parts.shape, jnp.float32),
            pltpu.VMEM(ratios.shape, jnp.float32),
            pltpu.VMEM(below.shape, jnp.float32),
            pltpu.SemaphoreType.DMA((rows // 8 + 2,)),
            pltpu.SemaphoreType.DMA((rows,)),
            pltpu.SemaphoreType.DMA((sea.shape[1],)),
        ],
        compiler_params=pltpu.CompilerParams(vmem_limit_bytes=LIMIT),
    )(parts, ratios, below, sea)


def body(
    air_state,
    mix_coef,
    flux_scale,
    sea_state,
    sea_rate,
    block_counts,
    cell_column,
    cell_owner,
    cell_coef,
    cell_weight,
    slot_cell,
    slot_frac,
):
    tracers, columns = air_state.shape[1:]
    ring = lax.axis_size("cols")
    rows = columns // BLOCK_COLS
    surf_cells = sea_state.shape[1]
    surf_rows = surf_cells // LANES
    capacity = slot_cell.shape[0] // (2 * ring)
    cap_rows = max(4, -(-capacity // LANES))

    parts, ratios, below, sea = forward(
        jnp.swapaxes(air_state, 0, 1),
        mix_coef,
        flux_scale.reshape(rows, LANES),
        sea_state,
        sea_rate.reshape(surf_rows, LANES),
        block_counts,
        cell_column.reshape(-1, LANES),
        cell_owner.reshape(-1, LANES),
        cell_coef.reshape(-1, LANES),
        cell_weight.reshape(-1, LANES),
        slot_cell.reshape(-1, LANES),
        slot_frac.reshape(-1, LANES),
        ring,
        cap_rows,
        capacity,
    )
    air_new, sea_new = ascend(parts, ratios, below, sea.reshape(tracers, surf_rows, LANES))
    return jnp.swapaxes(air_new, 0, 1), sea_new


def solution(mesh):
    return jax.shard_map(
        body,
        mesh=mesh,
        in_specs=(
            P("sect", None, "cols"),
            P("sect", "cols"),
            P("cols"),
            P(None, ("sect", "cols")),
            P(("sect", "cols")),
            P(("sect", "cols"), None),
            P(("sect", "cols")),
            P(("sect", "cols"), None),
            P(("sect", "cols")),
            P(("sect", "cols")),
            P(("sect", "cols")),
            P(("sect", "cols")),
        ),
        out_specs=(P("sect", None, "cols"), P(None, ("sect", "cols"))),
        check_vma=False,
    )
```

```python
import functools
import math

import jax
import jax.numpy as jnp
from jax import lax
from jax.experimental import pallas as pl
from jax.experimental.pallas import tpu as pltpu
from jax.sharding import PartitionSpec as P

BLOCK_COLS = 128
BLOCK_SLOTS = 256
SUBSTEPS = 2
GROUPS = 2
LANES = 128
LIMIT = 56 * 1024 * 1024
HBM = pl.BlockSpec(memory_space=pltpu.HBM)


def split(value):
    high = value.astype(jnp.bfloat16).astype(jnp.float32)
    return high, value - high


def hot(index, count):
    places = lax.broadcasted_iota(jnp.int32, (count, index.shape[1]), 0).astype(jnp.int16)
    return jnp.where(places == index.astype(jnp.int16), jnp.ones((), jnp.bfloat16), jnp.zeros((), jnp.bfloat16))


def in_line(packed):
    return jnp.concatenate([packed[r : r + 1] for r in range(packed.shape[0])], axis=1)


def in_rows(line):
    return jnp.concatenate([line[:, r : r + LANES] for r in range(0, line.shape[1], LANES)], axis=0)


def scatter(values, row, lane, rows):
    mask = hot(row, rows)
    parts = [split(value) for value in values]
    lines = [in_line(p[0]) for p in parts] + [in_line(p[1]) for p in parts]
    return lax.dot_general(
        jnp.concatenate([mask * line.astype(jnp.bfloat16) for line in lines], axis=0),
        hot(lane, LANES),
        (((1,), (1,)), ((), ())),
        preferred_element_type=jnp.float32,
    )


def table_of(value):
    high, low = split(value)
    return jnp.concatenate([high, low], axis=1).astype(jnp.bfloat16)


def gather(table, row, lane, rows):
    lane_hot = hot(lane, LANES)
    picked = jnp.dot(table, jnp.concatenate([lane_hot, lane_hot], axis=0), preferred_element_type=jnp.float32)
    mask = lax.broadcasted_iota(jnp.int32, (rows, row.shape[1]), 0) == row
    return [
        jnp.sum(jnp.where(mask, picked[q : q + rows], 0.0), axis=0, keepdims=True)
        for q in range(0, table.shape[0], rows)
    ]


def forward_kernel(
    tracers,
    ring,
    cap_rows,
    step_rows,
    capacity,
    air,
    mix,
    scale_in,
    sea_in,
    rate_in,
    counts_in,
    column_in,
    owner_in,
    coef_in,
    weight_in,
    cell_in,
    frac_in,
    parts_out,
    ratios_out,
    below_out,
    sea_new,
    parts,
    ratios,
    below,
    sea_out,
    scale,
    sea,
    rate,
    counts,
    column,
    owner,
    coef,
    weight,
    slot_cell,
    slot_frac,
    spots,
    mixes,
    inverses,
    hand,
    low,
    top,
    place_acc,
    offset,
    sorted_cells,
    cells,
    col_row,
    col_lane,
    flow,
    gain_sent,
    gain_came,
    strength,
    inverse,
    sent,
    arrived,
    back,
    returned,
    flux,
    flux_came,
    acc,
    send_sem,
    recv_sem,
    pair_send,
    pair_recv,
    local_sem,
    load_sem,
    fetch_sem,
    store_sem,
):
    levels, rows = ratios.shape[0], ratios.shape[1]
    surf_rows = rate.shape[0]
    devices = 2 * ring
    mine = tracers // GROUPS
    spot_rows = 2 * cap_rows
    sect = lax.axis_index("sect")
    me = lax.axis_index("cols")
    other = 1 - sect

    def ahead(s):
        return lax.rem(me + s, ring)

    def behind(s):
        return lax.rem(me + ring - s, ring)

    def remote(s):
        return not (isinstance(s, int) and s == 0)

    class Phase:
        def __init__(self, phase, source, target):
            self.phase, self.source, self.target = phase, source, target

        def copy(self, source, target, four, chip):
            return pltpu.make_async_remote_copy(
                src_ref=source,
                dst_ref=target,
                send_sem=send_sem.at[self.phase],
                recv_sem=recv_sem.at[self.phase, four],
                device_id=(sect, chip),
                device_id_type=pl.DeviceIdType.MESH,
            )

        def start(self, four, s):
            self.copy(self.source.at[ahead(s)], self.target.at[me], four, ahead(s)).start()

        def wait_four(self, four, steps):
            some = pl.ds(0, sum(remote(s) for s in steps))
            self.copy(self.source.at[some], self.target.at[some], four, ahead(1)).wait_recv()

        def wait_sent(self):
            some = pl.ds(0, ring - 1)
            self.copy(self.source.at[some], self.target.at[some], 0, ahead(1)).wait_send()

    gains = Phase(0, gain_sent, gain_came)

    def outward(step, g):
        return Phase(1 + 2 * (step * GROUPS + g), sent.at[g], arrived.at[g])

    def homeward(step, g):
        return Phase(2 + 2 * (step * GROUPS + g), back.at[g], returned.at[g])

    def to_partner(k, source, target):
        return pltpu.make_async_remote_copy(
            src_ref=source,
            dst_ref=target,
            send_sem=pair_send.at[k],
            recv_sem=pair_recv.at[k],
            device_id=(other, me),
            device_id_type=pl.DeviceIdType.MESH,
        )

    def flux_over(step, g):
        return to_partner(1 + step * GROUPS + g, flux.at[step, g], flux_came.at[step, g])

    def in_fours(act, order=0):
        def far(i, _):
            act(i, *[ring // 2 + 4 * i + j for j in range(4)])
            return 0

        def near(i, _):
            act(ring // 8 + i, *[ring // 2 - 1 - 4 * i - j for j in range(4)])
            return 0

        if order:
            act(ring // 4 - 1, 3, 2, 1, 0)
            lax.fori_loop(0, ring // 8 - 1, near, 0)
            lax.fori_loop(0, ring // 8, far, 0)
            return
        lax.fori_loop(0, ring // 8, far, 0)
        lax.fori_loop(0, ring // 8 - 1, near, 0)
        act(ring // 4 - 1, 3, 2, 1, 0)

    def line_of(ref, chips):
        return in_line(jnp.concatenate([ref[chip] for chip in chips], axis=0))

    def spot(v, chips):
        return in_line(
            jnp.concatenate(
                [spots[v, pl.ds(pl.multiple_of(chip * spot_rows, 8), spot_rows), :] for chip in chips], axis=0
            )
        ).astype(jnp.int32)

    barrier = pltpu.get_barrier_semaphore()

    def greet(s, _):
        pl.semaphore_signal(barrier, inc=1, device_id=(sect, ahead(s)), device_id_type=pl.DeviceIdType.MESH)
        return 0

    lax.fori_loop(1, ring, greet, 0)
    pl.semaphore_signal(barrier, inc=1, device_id=(other, me), device_id_type=pl.DeviceIdType.MESH)

    def load(j):
        here = pl.ds(pl.multiple_of(j * LANES, LANES), LANES)
        return [
            pltpu.make_async_copy(mix.at[:, here], mixes.at[:, j, :], load_sem.at[0, j]),
            pltpu.make_async_copy(air.at[:, :, here], parts.at[:, :, j, :], load_sem.at[1, j]),
        ]

    def start_load(j, _):
        for copy in load(j):
            copy.start()
        return 0

    def wait_load(j, _):
        for copy in load(j):
            copy.wait()
        return 0

    slot_rows = cell_in.shape[0]
    first_fetches = [(counts_in, counts), (owner_in, owner), (column_in, column), (coef_in, coef), (weight_in, weight)]
    later_fetches = [
        (scale_in, scale),
        (rate_in, rate),
        (cell_in, slot_cell.at[pl.ds(0, slot_rows)]),
        (frac_in, slot_frac.at[pl.ds(0, slot_rows)]),
    ]
    fetches = [
        pltpu.make_async_copy(source, target, fetch_sem.at[i])
        for i, (source, target) in enumerate(first_fetches + later_fetches)
    ]
    first_fetches, later_fetches = fetches[: len(first_fetches)], fetches[len(first_fetches) :]
    for copy in first_fetches:
        copy.start()
    lax.fori_loop(0, rows, start_load, 0)
    for copy in later_fetches:
        copy.start()

    def sea_part(j):
        here = pl.ds(pl.multiple_of(j * LANES, LANES), LANES)
        return pltpu.make_async_copy(sea_in.at[:, here], sea.at[:, j, :], load_sem.at[2, j])

    def start_sea(j, _):
        sea_part(j).start()
        return 0

    def wait_sea(j, _):
        sea_part(j).wait()
        return 0

    lax.fori_loop(0, surf_rows, start_sea, 0)
    for copy in first_fetches:
        copy.wait()
    block_of = lax.broadcasted_iota(jnp.int32, (owner.shape[0], counts.shape[1]), 0) // 2
    chosen = lax.broadcasted_iota(jnp.int32, (owner.shape[0], counts.shape[1]), 1) == block_of
    live = jnp.sum(jnp.where(chosen, counts[...].astype(jnp.float32), 0.0), axis=1, keepdims=True)
    places_in = lax.broadcasted_iota(jnp.int32, owner.shape, 1) + LANES * lax.rem(
        lax.broadcasted_iota(jnp.int32, owner.shape, 0), 2
    )
    coef[...] = jnp.where(places_in.astype(jnp.float32) < live, coef[...], 0.0)

    places = devices * cap_rows
    blocks = step_rows * LANES // BLOCK_SLOTS
    place_acc[...] = jnp.zeros_like(place_acc)
    offset[...] = jnp.zeros_like(offset)
    later = (
        lax.broadcasted_iota(jnp.int32, (BLOCK_SLOTS, BLOCK_SLOTS), 0)
        <= lax.broadcasted_iota(jnp.int32, (BLOCK_SLOTS, BLOCK_SLOTS), 1)
    )
    later = jnp.where(later, 1.0, 0.0).astype(jnp.bfloat16)
    numbers = lax.broadcasted_iota(jnp.int32, (step_rows, LANES), 0)

    def sort_part(i, _):
        here = pl.ds(pl.multiple_of(i * step_rows, step_rows), step_rows)
        own = in_line(owner[here, :])
        named = hot(own, devices)
        named_blocks = [named[:, b * BLOCK_SLOTS : (b + 1) * BLOCK_SLOTS] for b in range(blocks)]
        running = jnp.dot(jnp.concatenate(named_blocks, axis=0), later, preferred_element_type=jnp.float32)
        before = offset[...]
        ranks = []
        for b in range(blocks):
            wide = named_blocks[b].astype(jnp.float32)
            count = running[b * devices : (b + 1) * devices] + before[:, 0:1]
            ranks.append(jnp.sum(wide * count, axis=0, keepdims=True) - 1.0)
            before = before + jnp.broadcast_to(jnp.sum(wide, axis=1, keepdims=True), before.shape)
        offset[...] = before
        rank = jnp.concatenate(ranks, axis=1).astype(jnp.int32)
        gain = coef[here, :]
        gain_high, gain_low = split(gain)
        flow_high, flow_low = split(weight[here, :] * gain)
        values = [
            ((i * step_rows + numbers) // 2).astype(jnp.float32),
            column[here, :].astype(jnp.float32),
            gain_high,
            gain_low,
            flow_high,
            flow_low,
        ]
        mask = hot(lax.rem(own, ring) * cap_rows + rank // LANES, places // 2)
        lane = own // ring * LANES + lax.rem(rank, LANES)
        place_acc[...] += lax.dot_general(
            jnp.concatenate([mask * in_line(value).astype(jnp.bfloat16) for value in values], axis=0),
            hot(lane, 2 * LANES),
            (((1,), (1,)), ((), ())),
            preferred_element_type=jnp.float32,
        )
        return 0

    def eliminate(under):
        def coefficients(k, under):
            coupling = mixes[k]
            inv = 1.0 / (1.0 + coupling + under)
            ratio = coupling * inv
            inverses[k] = inv
            ratios[k] = ratio
            return ratio * (1.0 + under)

        return lax.fori_loop(0, levels, coefficients, under, unroll=4)

    def descend(carried_of, keep):
        for q in range(0, tracers, 2):

            def level(k, carried):
                ratio, inv = ratios[k], inverses[k]
                result = []
                for j, value in enumerate(carried):
                    value = parts[q + j, k] + value
                    parts[q + j, k] = value * inv
                    result.append(value * ratio)
                return result

            keep(q, lax.fori_loop(0, levels, level, [carried_of(q), carried_of(q + 1)], unroll=4))

    handed = to_partner(1 + SUBSTEPS * GROUPS, hand, hand)
    lowest = to_partner(2 + SUBSTEPS * GROUPS, low, low)
    highest = to_partner(3 + SUBSTEPS * GROUPS, top, top)
    upper, lower = sect == 0, sect == 1

    def piece(q):
        return slice(q * rows, (q + 1) * rows)

    sort_steps = owner.shape[0] // step_rows
    early = sort_steps // 3
    lax.fori_loop(0, early, sort_part, 0)
    pl.semaphore_wait(barrier, ring)
    lax.fori_loop(0, rows, wait_load, 0)
    later_fetches[0].wait()

    @pl.when(upper)
    def _():
        zero = jnp.zeros((rows, LANES), jnp.float32)
        hand[piece(tracers), :] = eliminate(zero)

        def keep(q, carried):
            hand[piece(q), :] = carried[0]
            hand[piece(q + 1), :] = carried[1]

        descend(lambda q: zero, keep)
        handed.start()

    lax.fori_loop(early, sort_steps, sort_part, 0)
    half = places // 2
    for d in range(2):
        rows_of, lanes_of = pl.ds(d * half, half), slice(d * LANES, (d + 1) * LANES)
        for v in range(2):
            sorted_cells[v, rows_of, :] = place_acc[v * half : (v + 1) * half, lanes_of]
            first = (2 + 2 * v) * half
            sorted_cells[2 + v, rows_of, :] = (
                place_acc[first : first + half, lanes_of] + place_acc[first + half : first + 2 * half, lanes_of]
            )

    def half_of(section):
        count = ring * cap_rows
        return sorted_cells.at[:, pl.ds(pl.multiple_of(section * count, 8), count), :]

    shared = to_partner(0, half_of(other), cells.at[sect])
    kept = pltpu.make_async_copy(half_of(sect), cells.at[sect], local_sem)
    shared.start()
    kept.start()

    @pl.when(lower)
    def _():
        handed.wait_recv()
        eliminate(hand[piece(tracers), :])
        ratios[levels - 1] = scale[...] * inverses[levels - 1]
        descend(lambda q: hand[piece(q), :], lambda q, carried: None)
        for q in range(tracers):
            low[piece(q), :] = parts[q, levels - 1]
        low[piece(tracers), :] = ratios[levels - 1]
        lowest.start()

    stores = [
        pltpu.make_async_copy(source, target, store_sem.at[i])
        for i, (source, target) in enumerate(
            [(parts, parts_out), (ratios, ratios_out), (sea_out, sea_new), (below, below_out)]
        )
    ]
    stores[0].start()
    stores[1].start()
    for copy in later_fetches[2:]:
        copy.wait()
    beyond = pl.ds(slot_rows, slot_cell.shape[0] - slot_rows)
    slot_cell[beyond, :] = jnp.zeros((slot_cell.shape[0] - slot_rows, LANES), jnp.int32)
    slot_frac[beyond, :] = jnp.zeros((slot_cell.shape[0] - slot_rows, LANES), jnp.float32)
    period = LANES // math.gcd(capacity, LANES)
    lane_numbers = lax.broadcasted_iota(jnp.int32, (cap_rows, LANES), 1)

    def cut(ref, row, shift):
        window = jnp.concatenate([ref[pl.ds(row + r, 1), :] for r in range(cap_rows + 1)], axis=0)
        if shift == 0:
            return window[:cap_rows]
        turned = pltpu.roll(window, LANES - shift, 1)
        return jnp.where(lane_numbers < LANES - shift, turned[:cap_rows], turned[1:])

    def place_spots(i, _):
        for j in range(period):
            source = i * period + j
            row = i * (period * capacity // LANES) + j * capacity // LANES
            cell = cut(slot_cell, row, j * capacity % LANES)
            frac = cut(slot_frac, row, j * capacity % LANES)
            start = lax.rem(source, ring) * spot_rows + source // ring * cap_rows
            for r in range(cap_rows):
                line = pl.ds(start + r, 1)
                spots[0, line, :] = (cell[r : r + 1] // LANES).astype(jnp.float32)
                spots[1, line, :] = lax.rem(cell[r : r + 1], LANES).astype(jnp.float32)
                spots[2, line, :] = frac[r : r + 1]
        return 0

    lax.fori_loop(0, devices // period, place_spots, 0)
    later_fetches[1].wait()
    lax.fori_loop(0, surf_rows, wait_sea, 0)
    kept.wait()
    shared.wait()

    def arrange(i, _):
        here = pl.ds(pl.multiple_of(i * spot_rows, 8), spot_rows)

        def merged(v, k):
            piece = slice(k * cap_rows, (k + 1) * cap_rows)
            return jnp.concatenate([cells[0, v, here, :][piece], cells[1, v, here, :][piece]], axis=0)

        for k in range(2):
            col_row[2 * i + k] = merged(0, k).astype(jnp.int32)
            col_lane[2 * i + k] = merged(1, k).astype(jnp.int32)
            gain_sent[2 * i + k] = merged(2, k)
            flow[2 * i + k] = merged(3, k)
        return 0

    lax.fori_loop(0, ring // 2, arrange, 0)

    def send_gain(four, *steps):
        for s in steps:
            if remote(s):
                gains.start(four, s)

    in_fours(send_gain)
    gain_came[me] = gain_sent[me]

    def send_all(step, g):
        here = slice(g * mine * rows, (g + 1) * mine * rows)
        bottom = low[here, :]
        if step:
            flux_over(step - 1, g).wait_recv()
            change = flux[step - 1, g] + flux_came[step - 1, g]
            bottom = bottom + jnp.concatenate([low[piece(tracers), :]] * mine, axis=0) * change
        table = table_of(bottom)

        def send(four, *steps):
            chips = [ahead(s) for s in steps]
            picked = [in_rows(p) for p in gather(table, line_of(col_row, chips), line_of(col_lane, chips), rows)]
            for j, (s, chip) in enumerate(zip(steps, chips)):
                sent[g, chip] = jnp.concatenate([p[j * spot_rows : (j + 1) * spot_rows] for p in picked], axis=0)
                if remote(s):
                    outward(step, g).start(four, s)

        in_fours(send, 1)
        arrived[g, me] = sent[g, me]

    def tally():
        acc[...] = jnp.zeros_like(acc)

        def receive(four, *steps):
            chips = [behind(s) for s in steps]
            gains.wait_four(four, steps)
            for chip in chips:
                here = pl.ds(pl.multiple_of(chip * spot_rows, 8), spot_rows)
                strength[chip] = gain_came[chip] * spots[2, here, :]
            force = jnp.concatenate([strength[chip] for chip in chips], axis=0)
            summed = scatter([force], spot(0, chips), spot(1, chips), surf_rows)
            acc[0:surf_rows] += summed[0:surf_rows] + summed[surf_rows:]

        in_fours(receive)
        inverse[...] = 1.0 / (1.0 + rate[...] * acc[0:surf_rows])

    def surface_all(step, g):
        acc[...] = jnp.zeros_like(acc)

        def receive(four, *steps):
            chips = [behind(s) for s in steps]
            outward(step, g).wait_four(four, steps)
            values = [
                jnp.concatenate(
                    [arrived[g, chip, q * spot_rows : (q + 1) * spot_rows, :] * strength[chip] for chip in chips],
                    axis=0,
                )
                for q in range(mine)
            ]
            summed = scatter(values, spot(0, chips), spot(1, chips), surf_rows)
            acc[...] += summed[0 : mine * surf_rows] + summed[mine * surf_rows :]

        in_fours(receive)
        for q in range(mine):
            here = slice(q * surf_rows, (q + 1) * surf_rows)
            there = slice((g * mine + q) * surf_rows, (g * mine + q + 1) * surf_rows)
            before = sea[g * mine + q] if step == 0 else sea_out[there, :]
            sea_out[there, :] = (before + rate[...] * acc[here, :]) * inverse[...]
        table = table_of(sea_out[g * mine * surf_rows : (g + 1) * mine * surf_rows, :])

        def give_back(four, *steps):
            chips = [ahead(s) for s in steps]
            picked = [in_rows(p) for p in gather(table, spot(0, chips), spot(1, chips), surf_rows)]
            for j, (s, chip) in enumerate(zip(steps, chips)):
                back[g, chip] = jnp.concatenate([p[j * spot_rows : (j + 1) * spot_rows] for p in picked], axis=0)
                if remote(s):
                    homeward(step, g).start(four, s)

        in_fours(give_back, 1)
        returned[g, me] = back[g, me]

    def take_all(step, g):
        flux[step, g] = jnp.zeros(flux.shape[2:], jnp.float32)

        def take_back(four, *steps):
            chips = [behind(s) for s in steps]
            homeward(step, g).wait_four(four, steps)
            values = []
            for q in range(mine):
                here = slice(q * spot_rows, (q + 1) * spot_rows)
                values.append(
                    jnp.concatenate(
                        [(returned[g, chip, here, :] - sent[g, chip, here, :]) * flow[chip] for chip in chips], axis=0
                    )
                )
            summed = scatter(values, line_of(col_row, chips), line_of(col_lane, chips), rows)
            flux[step, g] += summed[0 : mine * rows] + summed[mine * rows :]

        in_fours(take_back)
        flux_over(step, g).start()
        outward(step, g).wait_sent()
        homeward(step, g).wait_sent()

    @pl.when(upper)
    def _():
        handed.wait_send()
        lowest.wait_recv()

    for g in range(GROUPS):
        send_all(0, g)
    tally()

    @pl.when(lower)
    def _():
        for q in range(0, tracers, 2):

            def rise(i, values):
                k = levels - 2 - i
                return [parts[q + j, k] + ratios[k] * value for j, value in enumerate(values)]

            values = lax.fori_loop(0, levels - 1, rise, [parts[q + j, levels - 1] for j in range(2)], unroll=4)
            for j in range(2):
                top[piece(q + j), :] = values[j]
        top[piece(tracers), :] = lax.fori_loop(
            0, levels - 1, lambda i, value: value * ratios[levels - 2 - i], ratios[levels - 1], unroll=4
        )
        highest.start()

    for step in range(SUBSTEPS):
        for g in range(GROUPS):
            surface_all(step, g)
        for g in range(GROUPS):
            take_all(step, g)
        if step < SUBSTEPS - 1:
            for g in range(GROUPS):
                send_all(step + 1, g)

    stores[2].start()
    gains.wait_sent()

    @pl.when(lower)
    def _():
        lowest.wait_send()
        highest.wait_send()

    @pl.when(upper)
    def _():
        highest.wait_recv()

    for g in range(GROUPS):
        here = slice(g * mine * rows, (g + 1) * mine * rows)
        flux_over(SUBSTEPS - 1, g).wait_recv()
        below[here, :] = flux[SUBSTEPS - 1, g] + flux_came[SUBSTEPS - 1, g]

    @pl.when(upper)
    def _():
        for q in range(tracers):
            below[piece(q), :] = top[piece(q), :] + top[piece(tracers), :] * below[piece(q), :]

    stores[3].start()

    for step in range(SUBSTEPS):
        for g in range(GROUPS):
            flux_over(step, g).wait_send()
    for copy in stores:
        copy.wait()


def forward(air, mix, scale, sea, rate, counts, column, owner, coef, weight, cell, frac, ring, cap_rows, capacity):
    tracers, levels, _ = air.shape
    rows, surf_rows = scale.shape[0], rate.shape[0]
    mine = tracers // GROUPS
    places = 2 * ring * cap_rows
    step_rows = max(2, min(16, 2048 // places))
    while owner.shape[0] % step_rows:
        step_rows -= 2

    def real(*shape):
        return pltpu.VMEM(shape, jnp.float32)

    message = real(GROUPS, ring, mine * 2 * cap_rows, LANES)
    once = real(ring, 2 * cap_rows, LANES)
    column_state = real((tracers + 1) * rows, LANES)
    phases = 1 + 2 * SUBSTEPS * GROUPS
    return pl.pallas_call(
        functools.partial(forward_kernel, tracers, ring, cap_rows, step_rows, capacity),
        out_shape=[
            jax.ShapeDtypeStruct((tracers, levels, rows, LANES), jnp.float32),
            jax.ShapeDtypeStruct((levels, rows, LANES), jnp.float32),
            jax.ShapeDtypeStruct((tracers * rows, LANES), jnp.float32),
            jax.ShapeDtypeStruct((tracers * surf_rows, LANES), jnp.float32),
        ],
        in_specs=[HBM] * 12,
        out_specs=[HBM] * 4,
        scratch_shapes=[
            real(tracers, levels, rows, LANES),
            real(levels, rows, LANES),
            real(tracers * rows, LANES),
            real(tracers * surf_rows, LANES),
            real(rows, LANES),
            real(tracers, surf_rows, LANES),
            real(surf_rows, LANES),
            pltpu.VMEM(counts.shape, jnp.int32),
            pltpu.VMEM(column.shape, jnp.int32),
            pltpu.VMEM(owner.shape, jnp.int32),
            real(*coef.shape),
            real(*weight.shape),
            pltpu.VMEM((cell.shape[0] + 8, LANES), jnp.int32),
            real(frac.shape[0] + 8, LANES),
            real(3, ring * 2 * cap_rows, LANES),
            real(levels, rows, LANES),
            real(levels, rows, LANES),
            column_state,
            column_state,
            column_state,
            real(3 * places, 2 * LANES),
            real(2 * ring, LANES),
            real(4, places, LANES),
            real(2, 4, ring * cap_rows, LANES),
            pltpu.VMEM((ring, 2 * cap_rows, LANES), jnp.int32),
            pltpu.VMEM((ring, 2 * cap_rows, LANES), jnp.int32),
            once,
            once,
            once,
            once,
            real(surf_rows, LANES),
            message,
            message,
            message,
            message,
            real(SUBSTEPS, GROUPS, mine * rows, LANES),
            real(SUBSTEPS, GROUPS, mine * rows, LANES),
            real(mine * surf_rows, LANES),
            pltpu.SemaphoreType.DMA((phases,)),
            pltpu.SemaphoreType.DMA((phases, ring // 4)),
            pltpu.SemaphoreType.DMA((4 + SUBSTEPS * GROUPS,)),
            pltpu.SemaphoreType.DMA((4 + SUBSTEPS * GROUPS,)),
            pltpu.SemaphoreType.DMA,
            pltpu.SemaphoreType.DMA((3, rows)),
            pltpu.SemaphoreType.DMA((9,)),
            pltpu.SemaphoreType.DMA((4,)),
        ],
        compiler_params=pltpu.CompilerParams(
            vmem_limit_bytes=LIMIT, collective_id=0, has_side_effects=True
        ),
    )(air, mix, scale, sea, rate, counts, column, owner, coef, weight, cell, frac)


def ascend_kernel(parts_in, ratios_in, below_in, sea, out, sea_out, risen, ratios, below, load_sem, sem, sea_sem):
    tracers, levels, rows, _ = risen.shape
    tile = 8
    tiles = rows // tile

    def store_sea(j):
        here = pl.ds(pl.multiple_of(j * LANES, LANES), LANES)
        return pltpu.make_async_copy(sea.at[:, j, :], sea_out.at[:, here], sea_sem.at[j])

    def start_sea(j, _):
        store_sea(j).start()
        return 0

    def finish_sea(j, _):
        store_sea(j).wait()
        return 0

    def load(i):
        here = pl.ds(pl.multiple_of(i * tile, tile), tile)
        return pltpu.make_async_copy(parts_in.at[:, :, here, :], risen.at[:, :, here, :], load_sem.at[i])

    def store(j):
        here = pl.ds(pl.multiple_of(j * LANES, LANES), LANES)
        return pltpu.make_async_copy(risen.at[:, :, j, :], out.at[:, :, here], sem.at[j])

    firsts = [
        pltpu.make_async_copy(ratios_in, ratios, load_sem.at[tiles]),
        pltpu.make_async_copy(below_in, below, load_sem.at[tiles + 1]),
    ]
    load(0).start()
    for copy in firsts:
        copy.start()
    for i in range(1, tiles):
        load(i).start()
    lax.fori_loop(0, sea.shape[1], start_sea, 0)
    for copy in firsts:
        copy.wait()

    def columns(i, _):
        here = pl.ds(pl.multiple_of(i * tile, tile), tile)
        load(i).wait()

        def level(n, values):
            k = levels - 1 - n
            ratio = ratios[k, here, :]
            values = [risen[q, k, here, :] + ratio * value for q, value in enumerate(values)]
            for q, value in enumerate(values):
                risen[q, k, here, :] = value
            return values

        start = [below[pl.ds(pl.multiple_of(q * rows + i * tile, tile), tile), :] for q in range(tracers)]
        lax.fori_loop(0, levels, level, start, unroll=8)

        def send(j, _):
            store(i * tile + j).start()
            return 0

        lax.fori_loop(0, tile, send, 0)
        return 0

    lax.fori_loop(0, tiles, columns, 0)

    def finish(j, _):
        store(j).wait()
        return 0

    lax.fori_loop(0, rows, finish, 0)
    lax.fori_loop(0, sea.shape[1], finish_sea, 0)


def ascend(parts, ratios, below, sea):
    tracers, levels, rows, _ = parts.shape
    return pl.pallas_call(
        ascend_kernel,
        in_specs=[HBM] * 4,
        out_specs=[HBM] * 2,
        out_shape=[
            jax.ShapeDtypeStruct((tracers, levels, rows * LANES), jnp.float32),
            jax.ShapeDtypeStruct((tracers, sea.shape[1] * LANES), jnp.float32),
        ],
        scratch_shapes=[
            pltpu.VMEM(parts.shape, jnp.float32),
            pltpu.VMEM(ratios.shape, jnp.float32),
            pltpu.VMEM(below.shape, jnp.float32),
            pltpu.SemaphoreType.DMA((rows // 8 + 2,)),
            pltpu.SemaphoreType.DMA((rows,)),
            pltpu.SemaphoreType.DMA((sea.shape[1],)),
        ],
        compiler_params=pltpu.CompilerParams(vmem_limit_bytes=LIMIT),
    )(parts, ratios, below, sea)


def body(
    air_state,
    mix_coef,
    flux_scale,
    sea_state,
    sea_rate,
    block_counts,
    cell_column,
    cell_owner,
    cell_coef,
    cell_weight,
    slot_cell,
    slot_frac,
):
    tracers, columns = air_state.shape[1:]
    ring = lax.axis_size("cols")
    rows = columns // BLOCK_COLS
    surf_cells = sea_state.shape[1]
    surf_rows = surf_cells // LANES
    capacity = slot_cell.shape[0] // (2 * ring)
    cap_rows = max(4, -(-capacity // LANES))

    parts, ratios, below, sea = forward(
        jnp.swapaxes(air_state, 0, 1),
        mix_coef,
        flux_scale.reshape(rows, LANES),
        sea_state,
        sea_rate.reshape(surf_rows, LANES),
        block_counts,
        cell_column.reshape(-1, LANES),
        cell_owner.reshape(-1, LANES),
        cell_coef.reshape(-1, LANES),
        cell_weight.reshape(-1, LANES),
        slot_cell.reshape(-1, LANES),
        slot_frac.reshape(-1, LANES),
        ring,
        cap_rows,
        capacity,
    )
    air_new, sea_new = ascend(parts, ratios, below, sea.reshape(tracers, surf_rows, LANES))
    return jnp.swapaxes(air_new, 0, 1), sea_new


def solution(mesh):
    return jax.shard_map(
        body,
        mesh=mesh,
        in_specs=(
            P("sect", None, "cols"),
            P("sect", "cols"),
            P("cols"),
            P(None, ("sect", "cols")),
            P(("sect", "cols")),
            P(("sect", "cols"), None),
            P(("sect", "cols")),
            P(("sect", "cols"), None),
            P(("sect", "cols")),
            P(("sect", "cols")),
            P(("sect", "cols")),
            P(("sect", "cols")),
        ),
        out_specs=(P("sect", None, "cols"), P(None, ("sect", "cols"))),
        check_vma=False,
    )
```

```python
import functools
import math

import jax
import jax.numpy as jnp
from jax import lax
from jax.experimental import pallas as pl
from jax.experimental.pallas import tpu as pltpu
from jax.sharding import PartitionSpec as P

BLOCK_COLS = 128
BLOCK_SLOTS = 256
SUBSTEPS = 2
GROUPS = 2
LANES = 128
LIMIT = 56 * 1024 * 1024
HBM = pl.BlockSpec(memory_space=pltpu.HBM)


def split(value):
    high = value.astype(jnp.bfloat16).astype(jnp.float32)
    return high, value - high


def hot(index, count):
    places = lax.broadcasted_iota(jnp.int32, (count, index.shape[1]), 0).astype(jnp.int16)
    return jnp.where(places == index.astype(jnp.int16), jnp.ones((), jnp.bfloat16), jnp.zeros((), jnp.bfloat16))


def in_line(packed):
    return jnp.concatenate([packed[r : r + 1] for r in range(packed.shape[0])], axis=1)


def in_rows(line):
    return jnp.concatenate([line[:, r : r + LANES] for r in range(0, line.shape[1], LANES)], axis=0)


def scatter(values, row, lane, rows):
    mask = hot(row, rows)
    parts = [split(value) for value in values]
    lines = [in_line(p[0]) for p in parts] + [in_line(p[1]) for p in parts]
    return lax.dot_general(
        jnp.concatenate([mask * line.astype(jnp.bfloat16) for line in lines], axis=0),
        hot(lane, LANES),
        (((1,), (1,)), ((), ())),
        preferred_element_type=jnp.float32,
    )


def table_of(value):
    high, low = split(value)
    return jnp.concatenate([high, low], axis=1).astype(jnp.bfloat16)


def gather(table, row, lane, rows):
    lane_hot = hot(lane, LANES)
    picked = jnp.dot(table, jnp.concatenate([lane_hot, lane_hot], axis=0), preferred_element_type=jnp.float32)
    mask = lax.broadcasted_iota(jnp.int32, (rows, row.shape[1]), 0) == row
    return [
        jnp.sum(jnp.where(mask, picked[q : q + rows], 0.0), axis=0, keepdims=True)
        for q in range(0, table.shape[0], rows)
    ]


def forward_kernel(
    tracers,
    ring,
    cap_rows,
    step_rows,
    capacity,
    air,
    mix,
    scale_in,
    sea_in,
    rate_in,
    counts_in,
    column_in,
    owner_in,
    coef_in,
    weight_in,
    cell_in,
    frac_in,
    parts_out,
    ratios_out,
    below_out,
    sea_new,
    parts,
    ratios,
    below,
    sea_out,
    scale,
    sea,
    rate,
    counts,
    column,
    owner,
    coef,
    weight,
    slot_cell,
    slot_frac,
    spots,
    mixes,
    inverses,
    hand,
    low,
    top,
    place_acc,
    offset,
    sorted_cells,
    cells,
    col_row,
    col_lane,
    flow,
    gain_sent,
    gain_came,
    strength,
    inverse,
    sent,
    arrived,
    back,
    returned,
    flux,
    flux_came,
    acc,
    send_sem,
    recv_sem,
    pair_send,
    pair_recv,
    local_sem,
    load_sem,
    fetch_sem,
    store_sem,
):
    levels, rows = ratios.shape[0], ratios.shape[1]
    surf_rows = rate.shape[0]
    devices = 2 * ring
    mine = tracers // GROUPS
    spot_rows = 2 * cap_rows
    sect = lax.axis_index("sect")
    me = lax.axis_index("cols")
    other = 1 - sect

    def ahead(s):
        return lax.rem(me + s, ring)

    def behind(s):
        return lax.rem(me + ring - s, ring)

    def remote(s):
        return not (isinstance(s, int) and s == 0)

    class Phase:
        def __init__(self, phase, source, target):
            self.phase, self.source, self.target = phase, source, target

        def copy(self, source, target, four, chip):
            return pltpu.make_async_remote_copy(
                src_ref=source,
                dst_ref=target,
                send_sem=send_sem.at[self.phase],
                recv_sem=recv_sem.at[self.phase, four],
                device_id=(sect, chip),
                device_id_type=pl.DeviceIdType.MESH,
            )

        def start(self, four, s):
            self.copy(self.source.at[ahead(s)], self.target.at[me], four, ahead(s)).start()

        def wait_four(self, four, steps):
            some = pl.ds(0, sum(remote(s) for s in steps))
            self.copy(self.source.at[some], self.target.at[some], four, ahead(1)).wait_recv()

        def wait_sent(self):
            some = pl.ds(0, ring - 1)
            self.copy(self.source.at[some], self.target.at[some], 0, ahead(1)).wait_send()

    gains = Phase(0, gain_sent, gain_came)

    def outward(step, g):
        return Phase(1 + 2 * (step * GROUPS + g), sent.at[g], arrived.at[g])

    def homeward(step, g):
        return Phase(2 + 2 * (step * GROUPS + g), back.at[g], returned.at[g])

    def to_partner(k, source, target):
        return pltpu.make_async_remote_copy(
            src_ref=source,
            dst_ref=target,
            send_sem=pair_send.at[k],
            recv_sem=pair_recv.at[k],
            device_id=(other, me),
            device_id_type=pl.DeviceIdType.MESH,
        )

    def flux_over(step, g):
        return to_partner(1 + step * GROUPS + g, flux.at[step, g], flux_came.at[step, g])

    def in_fours(act, order=0):
        def far(i, _):
            act(i, *[ring // 2 + 4 * i + j for j in range(4)])
            return 0

        def near(i, _):
            act(ring // 8 + i, *[ring // 2 - 1 - 4 * i - j for j in range(4)])
            return 0

        if order:
            act(ring // 4 - 1, 3, 2, 1, 0)
            lax.fori_loop(0, ring // 8 - 1, near, 0)
            lax.fori_loop(0, ring // 8, far, 0)
            return
        lax.fori_loop(0, ring // 8, far, 0)
        lax.fori_loop(0, ring // 8 - 1, near, 0)
        act(ring // 4 - 1, 3, 2, 1, 0)

    def line_of(ref, chips):
        return in_line(jnp.concatenate([ref[chip] for chip in chips], axis=0))

    def spot(v, chips):
        return in_line(
            jnp.concatenate(
                [spots[v, pl.ds(pl.multiple_of(chip * spot_rows, 8), spot_rows), :] for chip in chips], axis=0
            )
        ).astype(jnp.int32)

    barrier = pltpu.get_barrier_semaphore()

    def greet(s, _):
        pl.semaphore_signal(barrier, inc=1, device_id=(sect, ahead(s)), device_id_type=pl.DeviceIdType.MESH)
        return 0

    lax.fori_loop(1, ring, greet, 0)
    pl.semaphore_signal(barrier, inc=1, device_id=(other, me), device_id_type=pl.DeviceIdType.MESH)

    def load(j):
        here = pl.ds(pl.multiple_of(j * LANES, LANES), LANES)
        return [
            pltpu.make_async_copy(mix.at[:, here], mixes.at[:, j, :], load_sem.at[0, j]),
            pltpu.make_async_copy(air.at[:, :, here], parts.at[:, :, j, :], load_sem.at[1, j]),
        ]

    def start_load(j, _):
        for copy in load(j):
            copy.start()
        return 0

    def wait_load(j, _):
        for copy in load(j):
            copy.wait()
        return 0

    slot_rows = cell_in.shape[0]
    first_fetches = [(counts_in, counts), (owner_in, owner), (column_in, column), (coef_in, coef), (weight_in, weight)]
    later_fetches = [
        (scale_in, scale),
        (rate_in, rate),
        (cell_in, slot_cell.at[pl.ds(0, slot_rows)]),
        (frac_in, slot_frac.at[pl.ds(0, slot_rows)]),
    ]
    fetches = [
        pltpu.make_async_copy(source, target, fetch_sem.at[i])
        for i, (source, target) in enumerate(first_fetches + later_fetches)
    ]
    first_fetches, later_fetches = fetches[: len(first_fetches)], fetches[len(first_fetches) :]
    for copy in first_fetches:
        copy.start()
    lax.fori_loop(0, rows, start_load, 0)
    for copy in later_fetches:
        copy.start()

    def sea_part(j):
        here = pl.ds(pl.multiple_of(j * LANES, LANES), LANES)
        return pltpu.make_async_copy(sea_in.at[:, here], sea.at[:, j, :], load_sem.at[2, j])

    def start_sea(j, _):
        sea_part(j).start()
        return 0

    def wait_sea(j, _):
        sea_part(j).wait()
        return 0

    lax.fori_loop(0, surf_rows, start_sea, 0)
    for copy in first_fetches:
        copy.wait()
    block_of = lax.broadcasted_iota(jnp.int32, (owner.shape[0], counts.shape[1]), 0) // 2
    chosen = lax.broadcasted_iota(jnp.int32, (owner.shape[0], counts.shape[1]), 1) == block_of
    live = jnp.sum(jnp.where(chosen, counts[...].astype(jnp.float32), 0.0), axis=1, keepdims=True)
    places_in = lax.broadcasted_iota(jnp.int32, owner.shape, 1) + LANES * lax.rem(
        lax.broadcasted_iota(jnp.int32, owner.shape, 0), 2
    )
    coef[...] = jnp.where(places_in.astype(jnp.float32) < live, coef[...], 0.0)

    places = devices * cap_rows
    blocks = step_rows * LANES // BLOCK_SLOTS
    place_acc[...] = jnp.zeros_like(place_acc)
    offset[...] = jnp.zeros_like(offset)
    later = (
        lax.broadcasted_iota(jnp.int32, (BLOCK_SLOTS, BLOCK_SLOTS), 0)
        <= lax.broadcasted_iota(jnp.int32, (BLOCK_SLOTS, BLOCK_SLOTS), 1)
    )
    later = jnp.where(later, 1.0, 0.0).astype(jnp.bfloat16)
    numbers = lax.broadcasted_iota(jnp.int32, (step_rows, LANES), 0)

    def sort_part(i, _):
        here = pl.ds(pl.multiple_of(i * step_rows, step_rows), step_rows)
        own = in_line(owner[here, :])
        named = hot(own, devices)
        named_blocks = [named[:, b * BLOCK_SLOTS : (b + 1) * BLOCK_SLOTS] for b in range(blocks)]
        running = jnp.dot(jnp.concatenate(named_blocks, axis=0), later, preferred_element_type=jnp.float32)
        before = offset[...]
        ranks = []
        for b in range(blocks):
            wide = named_blocks[b].astype(jnp.float32)
            count = running[b * devices : (b + 1) * devices] + before[:, 0:1]
            ranks.append(jnp.sum(wide * count, axis=0, keepdims=True) - 1.0)
            before = before + jnp.broadcast_to(jnp.sum(wide, axis=1, keepdims=True), before.shape)
        offset[...] = before
        rank = jnp.concatenate(ranks, axis=1).astype(jnp.int32)
        gain = coef[here, :]
        gain_high, gain_low = split(gain)
        flow_high, flow_low = split(weight[here, :] * gain)
        values = [
            ((i * step_rows + numbers) // 2).astype(jnp.float32),
            column[here, :].astype(jnp.float32),
            gain_high,
            gain_low,
            flow_high,
            flow_low,
        ]
        mask = hot(lax.rem(own, ring) * cap_rows + rank // LANES, places // 2)
        lane = own // ring * LANES + lax.rem(rank, LANES)
        place_acc[...] += lax.dot_general(
            jnp.concatenate([mask * in_line(value).astype(jnp.bfloat16) for value in values], axis=0),
            hot(lane, 2 * LANES),
            (((1,), (1,)), ((), ())),
            preferred_element_type=jnp.float32,
        )
        return 0

    def eliminate(under):
        def coefficients(k, under):
            coupling = mixes[k]
            inv = 1.0 / (1.0 + coupling + under)
            ratio = coupling * inv
            inverses[k] = inv
            ratios[k] = ratio
            return ratio * (1.0 + under)

        return lax.fori_loop(0, levels, coefficients, under, unroll=4)

    def descend(carried_of, keep):
        for q in range(0, tracers, 2):

            def level(k, carried):
                ratio, inv = ratios[k], inverses[k]
                result = []
                for j, value in enumerate(carried):
                    value = parts[q + j, k] + value
                    parts[q + j, k] = value * inv
                    result.append(value * ratio)
                return result

            keep(q, lax.fori_loop(0, levels, level, [carried_of(q), carried_of(q + 1)], unroll=4))

    handed = to_partner(1 + SUBSTEPS * GROUPS, hand, hand)
    lowest = to_partner(2 + SUBSTEPS * GROUPS, low, low)
    highest = to_partner(3 + SUBSTEPS * GROUPS, top, top)
    upper, lower = sect == 0, sect == 1

    def piece(q):
        return slice(q * rows, (q + 1) * rows)

    sort_steps = owner.shape[0] // step_rows
    early = sort_steps // 3
    lax.fori_loop(0, early, sort_part, 0)
    pl.semaphore_wait(barrier, ring)
    lax.fori_loop(0, rows, wait_load, 0)
    later_fetches[0].wait()

    @pl.when(upper)
    def _():
        zero = jnp.zeros((rows, LANES), jnp.float32)
        hand[piece(tracers), :] = eliminate(zero)

        def keep(q, carried):
            hand[piece(q), :] = carried[0]
            hand[piece(q + 1), :] = carried[1]

        descend(lambda q: zero, keep)
        handed.start()

    lax.fori_loop(early, sort_steps, sort_part, 0)
    half = places // 2
    for d in range(2):
        rows_of, lanes_of = pl.ds(d * half, half), slice(d * LANES, (d + 1) * LANES)
        for v in range(2):
            sorted_cells[v, rows_of, :] = place_acc[v * half : (v + 1) * half, lanes_of]
            first = (2 + 2 * v) * half
            sorted_cells[2 + v, rows_of, :] = (
                place_acc[first : first + half, lanes_of] + place_acc[first + half : first + 2 * half, lanes_of]
            )

    def half_of(section):
        count = ring * cap_rows
        return sorted_cells.at[:, pl.ds(pl.multiple_of(section * count, 8), count), :]

    shared = to_partner(0, half_of(other), cells.at[sect])
    kept = pltpu.make_async_copy(half_of(sect), cells.at[sect], local_sem)
    shared.start()
    kept.start()

    @pl.when(lower)
    def _():
        handed.wait_recv()
        eliminate(hand[piece(tracers), :])
        ratios[levels - 1] = scale[...] * inverses[levels - 1]
        descend(lambda q: hand[piece(q), :], lambda q, carried: None)
        for q in range(tracers):
            low[piece(q), :] = parts[q, levels - 1]
        low[piece(tracers), :] = ratios[levels - 1]
        lowest.start()

    stores = [
        pltpu.make_async_copy(source, target, store_sem.at[i])
        for i, (source, target) in enumerate(
            [(parts, parts_out), (ratios, ratios_out), (sea_out, sea_new), (below, below_out)]
        )
    ]
    stores[0].start()
    stores[1].start()
    for copy in later_fetches[2:]:
        copy.wait()
    beyond = pl.ds(slot_rows, slot_cell.shape[0] - slot_rows)
    slot_cell[beyond, :] = jnp.zeros((slot_cell.shape[0] - slot_rows, LANES), jnp.int32)
    slot_frac[beyond, :] = jnp.zeros((slot_cell.shape[0] - slot_rows, LANES), jnp.float32)
    period = LANES // math.gcd(capacity, LANES)
    lane_numbers = lax.broadcasted_iota(jnp.int32, (cap_rows, LANES), 1)

    def cut(ref, row, shift):
        window = jnp.concatenate([ref[pl.ds(row + r, 1), :] for r in range(cap_rows + 1)], axis=0)
        if shift == 0:
            return window[:cap_rows]
        turned = pltpu.roll(window, LANES - shift, 1)
        return jnp.where(lane_numbers < LANES - shift, turned[:cap_rows], turned[1:])

    def place_spots(i, _):
        for j in range(period):
            source = i * period + j
            row = i * (period * capacity // LANES) + j * capacity // LANES
            cell = cut(slot_cell, row, j * capacity % LANES)
            frac = cut(slot_frac, row, j * capacity % LANES)
            start = lax.rem(source, ring) * spot_rows + source // ring * cap_rows
            for r in range(cap_rows):
                line = pl.ds(start + r, 1)
                spots[0, line, :] = (cell[r : r + 1] // LANES).astype(jnp.float32)
                spots[1, line, :] = lax.rem(cell[r : r + 1], LANES).astype(jnp.float32)
                spots[2, line, :] = frac[r : r + 1]
        return 0

    lax.fori_loop(0, devices // period, place_spots, 0)
    later_fetches[1].wait()
    lax.fori_loop(0, surf_rows, wait_sea, 0)
    kept.wait()
    shared.wait()

    def arrange(i, _):
        here = pl.ds(pl.multiple_of(i * spot_rows, 8), spot_rows)

        def merged(v, k):
            piece = slice(k * cap_rows, (k + 1) * cap_rows)
            return jnp.concatenate([cells[0, v, here, :][piece], cells[1, v, here, :][piece]], axis=0)

        for k in range(2):
            col_row[2 * i + k] = merged(0, k).astype(jnp.int32)
            col_lane[2 * i + k] = merged(1, k).astype(jnp.int32)
            gain_sent[2 * i + k] = merged(2, k)
            flow[2 * i + k] = merged(3, k)
        return 0

    lax.fori_loop(0, ring // 2, arrange, 0)

    def send_gain(four, *steps):
        for s in steps:
            if remote(s):
                gains.start(four, s)

    in_fours(send_gain)
    gain_came[me] = gain_sent[me]

    def send_all(step, g):
        here = slice(g * mine * rows, (g + 1) * mine * rows)
        bottom = low[here, :]
        if step:
            flux_over(step - 1, g).wait_recv()
            change = flux[step - 1, g] + flux_came[step - 1, g]
            bottom = bottom + jnp.concatenate([low[piece(tracers), :]] * mine, axis=0) * change
        table = table_of(bottom)

        def send(four, *steps):
            chips = [ahead(s) for s in steps]
            picked = [in_rows(p) for p in gather(table, line_of(col_row, chips), line_of(col_lane, chips), rows)]
            for j, (s, chip) in enumerate(zip(steps, chips)):
                sent[g, chip] = jnp.concatenate([p[j * spot_rows : (j + 1) * spot_rows] for p in picked], axis=0)
                if remote(s):
                    outward(step, g).start(four, s)

        in_fours(send, 1)
        arrived[g, me] = sent[g, me]

    def tally():
        acc[...] = jnp.zeros_like(acc)

        def receive(four, *steps):
            chips = [behind(s) for s in steps]
            gains.wait_four(four, steps)
            for chip in chips:
                here = pl.ds(pl.multiple_of(chip * spot_rows, 8), spot_rows)
                strength[chip] = gain_came[chip] * spots[2, here, :]
            force = jnp.concatenate([strength[chip] for chip in chips], axis=0)
            summed = scatter([force], spot(0, chips), spot(1, chips), surf_rows)
            acc[0:surf_rows] += summed[0:surf_rows] + summed[surf_rows:]

        in_fours(receive, 1)
        inverse[...] = 1.0 / (1.0 + rate[...] * acc[0:surf_rows])

    def surface_all(step, g):
        acc[...] = jnp.zeros_like(acc)

        def receive(four, *steps):
            chips = [behind(s) for s in steps]
            outward(step, g).wait_four(four, steps)
            values = [
                jnp.concatenate(
                    [arrived[g, chip, q * spot_rows : (q + 1) * spot_rows, :] * strength[chip] for chip in chips],
                    axis=0,
                )
                for q in range(mine)
            ]
            summed = scatter(values, spot(0, chips), spot(1, chips), surf_rows)
            acc[...] += summed[0 : mine * surf_rows] + summed[mine * surf_rows :]

        in_fours(receive, 1)
        for q in range(mine):
            here = slice(q * surf_rows, (q + 1) * surf_rows)
            there = slice((g * mine + q) * surf_rows, (g * mine + q + 1) * surf_rows)
            before = sea[g * mine + q] if step == 0 else sea_out[there, :]
            sea_out[there, :] = (before + rate[...] * acc[here, :]) * inverse[...]
        table = table_of(sea_out[g * mine * surf_rows : (g + 1) * mine * surf_rows, :])

        def give_back(four, *steps):
            chips = [ahead(s) for s in steps]
            picked = [in_rows(p) for p in gather(table, spot(0, chips), spot(1, chips), surf_rows)]
            for j, (s, chip) in enumerate(zip(steps, chips)):
                back[g, chip] = jnp.concatenate([p[j * spot_rows : (j + 1) * spot_rows] for p in picked], axis=0)
                if remote(s):
                    homeward(step, g).start(four, s)

        in_fours(give_back, 1)
        returned[g, me] = back[g, me]

    def take_all(step, g):
        flux[step, g] = jnp.zeros(flux.shape[2:], jnp.float32)

        def take_back(four, *steps):
            chips = [behind(s) for s in steps]
            homeward(step, g).wait_four(four, steps)
            values = []
            for q in range(mine):
                here = slice(q * spot_rows, (q + 1) * spot_rows)
                values.append(
                    jnp.concatenate(
                        [(returned[g, chip, here, :] - sent[g, chip, here, :]) * flow[chip] for chip in chips], axis=0
                    )
                )
            summed = scatter(values, line_of(col_row, chips), line_of(col_lane, chips), rows)
            flux[step, g] += summed[0 : mine * rows] + summed[mine * rows :]

        in_fours(take_back, 1)
        flux_over(step, g).start()
        outward(step, g).wait_sent()
        homeward(step, g).wait_sent()

    @pl.when(upper)
    def _():
        handed.wait_send()
        lowest.wait_recv()

    for g in range(GROUPS):
        send_all(0, g)
    tally()

    @pl.when(lower)
    def _():
        for q in range(0, tracers, 2):

            def rise(i, values):
                k = levels - 2 - i
                return [parts[q + j, k] + ratios[k] * value for j, value in enumerate(values)]

            values = lax.fori_loop(0, levels - 1, rise, [parts[q + j, levels - 1] for j in range(2)], unroll=4)
            for j in range(2):
                top[piece(q + j), :] = values[j]
        top[piece(tracers), :] = lax.fori_loop(
            0, levels - 1, lambda i, value: value * ratios[levels - 2 - i], ratios[levels - 1], unroll=4
        )
        highest.start()

    for step in range(SUBSTEPS):
        for g in range(GROUPS):
            surface_all(step, g)
        for g in range(GROUPS):
            take_all(step, g)
        if step < SUBSTEPS - 1:
            for g in range(GROUPS):
                send_all(step + 1, g)

    stores[2].start()
    gains.wait_sent()

    @pl.when(lower)
    def _():
        lowest.wait_send()
        highest.wait_send()

    @pl.when(upper)
    def _():
        highest.wait_recv()

    for g in range(GROUPS):
        here = slice(g * mine * rows, (g + 1) * mine * rows)
        flux_over(SUBSTEPS - 1, g).wait_recv()
        below[here, :] = flux[SUBSTEPS - 1, g] + flux_came[SUBSTEPS - 1, g]

    @pl.when(upper)
    def _():
        for q in range(tracers):
            below[piece(q), :] = top[piece(q), :] + top[piece(tracers), :] * below[piece(q), :]

    stores[3].start()

    for step in range(SUBSTEPS):
        for g in range(GROUPS):
            flux_over(step, g).wait_send()
    for copy in stores:
        copy.wait()


def forward(air, mix, scale, sea, rate, counts, column, owner, coef, weight, cell, frac, ring, cap_rows, capacity):
    tracers, levels, _ = air.shape
    rows, surf_rows = scale.shape[0], rate.shape[0]
    mine = tracers // GROUPS
    places = 2 * ring * cap_rows
    step_rows = max(2, min(32, 4096 // places))
    while owner.shape[0] % step_rows:
        step_rows -= 2

    def real(*shape):
        return pltpu.VMEM(shape, jnp.float32)

    message = real(GROUPS, ring, mine * 2 * cap_rows, LANES)
    once = real(ring, 2 * cap_rows, LANES)
    column_state = real((tracers + 1) * rows, LANES)
    phases = 1 + 2 * SUBSTEPS * GROUPS
    return pl.pallas_call(
        functools.partial(forward_kernel, tracers, ring, cap_rows, step_rows, capacity),
        out_shape=[
            jax.ShapeDtypeStruct((tracers, levels, rows, LANES), jnp.float32),
            jax.ShapeDtypeStruct((levels, rows, LANES), jnp.float32),
            jax.ShapeDtypeStruct((tracers * rows, LANES), jnp.float32),
            jax.ShapeDtypeStruct((tracers * surf_rows, LANES), jnp.float32),
        ],
        in_specs=[HBM] * 12,
        out_specs=[HBM] * 4,
        scratch_shapes=[
            real(tracers, levels, rows, LANES),
            real(levels, rows, LANES),
            real(tracers * rows, LANES),
            real(tracers * surf_rows, LANES),
            real(rows, LANES),
            real(tracers, surf_rows, LANES),
            real(surf_rows, LANES),
            pltpu.VMEM(counts.shape, jnp.int32),
            pltpu.VMEM(column.shape, jnp.int32),
            pltpu.VMEM(owner.shape, jnp.int32),
            real(*coef.shape),
            real(*weight.shape),
            pltpu.VMEM((cell.shape[0] + 8, LANES), jnp.int32),
            real(frac.shape[0] + 8, LANES),
            real(3, ring * 2 * cap_rows, LANES),
            real(levels, rows, LANES),
            real(levels, rows, LANES),
            column_state,
            column_state,
            column_state,
            real(3 * places, 2 * LANES),
            real(2 * ring, LANES),
            real(4, places, LANES),
            real(2, 4, ring * cap_rows, LANES),
            pltpu.VMEM((ring, 2 * cap_rows, LANES), jnp.int32),
            pltpu.VMEM((ring, 2 * cap_rows, LANES), jnp.int32),
            once,
            once,
            once,
            once,
            real(surf_rows, LANES),
            message,
            message,
            message,
            message,
            real(SUBSTEPS, GROUPS, mine * rows, LANES),
            real(SUBSTEPS, GROUPS, mine * rows, LANES),
            real(mine * surf_rows, LANES),
            pltpu.SemaphoreType.DMA((phases,)),
            pltpu.SemaphoreType.DMA((phases, ring // 4)),
            pltpu.SemaphoreType.DMA((4 + SUBSTEPS * GROUPS,)),
            pltpu.SemaphoreType.DMA((4 + SUBSTEPS * GROUPS,)),
            pltpu.SemaphoreType.DMA,
            pltpu.SemaphoreType.DMA((3, rows)),
            pltpu.SemaphoreType.DMA((9,)),
            pltpu.SemaphoreType.DMA((4,)),
        ],
        compiler_params=pltpu.CompilerParams(
            vmem_limit_bytes=LIMIT, collective_id=0, has_side_effects=True
        ),
    )(air, mix, scale, sea, rate, counts, column, owner, coef, weight, cell, frac)


def ascend_kernel(parts_in, ratios_in, below_in, sea, out, sea_out, risen, ratios, below, load_sem, sem, sea_sem):
    tracers, levels, rows, _ = risen.shape
    tile = 16
    tiles = rows // tile

    def store_sea(j):
        here = pl.ds(pl.multiple_of(j * LANES, LANES), LANES)
        return pltpu.make_async_copy(sea.at[:, j, :], sea_out.at[:, here], sea_sem.at[j])

    def start_sea(j, _):
        store_sea(j).start()
        return 0

    def finish_sea(j, _):
        store_sea(j).wait()
        return 0

    def load(i):
        here = pl.ds(pl.multiple_of(i * tile, tile), tile)
        return pltpu.make_async_copy(parts_in.at[:, :, here, :], risen.at[:, :, here, :], load_sem.at[i])

    def store(j):
        here = pl.ds(pl.multiple_of(j * LANES, LANES), LANES)
        return pltpu.make_async_copy(risen.at[:, :, j, :], out.at[:, :, here], sem.at[j])

    firsts = [
        pltpu.make_async_copy(ratios_in, ratios, load_sem.at[tiles]),
        pltpu.make_async_copy(below_in, below, load_sem.at[tiles + 1]),
    ]
    load(0).start()
    for copy in firsts:
        copy.start()
    for i in range(1, tiles):
        load(i).start()
    lax.fori_loop(0, sea.shape[1], start_sea, 0)
    for copy in firsts:
        copy.wait()

    def columns(i, _):
        here = pl.ds(pl.multiple_of(i * tile, tile), tile)
        load(i).wait()

        def level(n, values):
            k = levels - 1 - n
            ratio = ratios[k, here, :]
            values = [risen[q, k, here, :] + ratio * value for q, value in enumerate(values)]
            for q, value in enumerate(values):
                risen[q, k, here, :] = value
            return values

        start = [below[pl.ds(pl.multiple_of(q * rows + i * tile, tile), tile), :] for q in range(tracers)]
        lax.fori_loop(0, levels, level, start, unroll=8)

        def send(j, _):
            store(i * tile + j).start()
            return 0

        lax.fori_loop(0, tile, send, 0)
        return 0

    lax.fori_loop(0, tiles, columns, 0)

    def finish(j, _):
        store(j).wait()
        return 0

    lax.fori_loop(0, rows, finish, 0)
    lax.fori_loop(0, sea.shape[1], finish_sea, 0)


def ascend(parts, ratios, below, sea):
    tracers, levels, rows, _ = parts.shape
    return pl.pallas_call(
        ascend_kernel,
        in_specs=[HBM] * 4,
        out_specs=[HBM] * 2,
        out_shape=[
            jax.ShapeDtypeStruct((tracers, levels, rows * LANES), jnp.float32),
            jax.ShapeDtypeStruct((tracers, sea.shape[1] * LANES), jnp.float32),
        ],
        scratch_shapes=[
            pltpu.VMEM(parts.shape, jnp.float32),
            pltpu.VMEM(ratios.shape, jnp.float32),
            pltpu.VMEM(below.shape, jnp.float32),
            pltpu.SemaphoreType.DMA((rows // 16 + 2,)),
            pltpu.SemaphoreType.DMA((rows,)),
            pltpu.SemaphoreType.DMA((sea.shape[1],)),
        ],
        compiler_params=pltpu.CompilerParams(vmem_limit_bytes=LIMIT),
    )(parts, ratios, below, sea)


def body(
    air_state,
    mix_coef,
    flux_scale,
    sea_state,
    sea_rate,
    block_counts,
    cell_column,
    cell_owner,
    cell_coef,
    cell_weight,
    slot_cell,
    slot_frac,
):
    tracers, columns = air_state.shape[1:]
    ring = lax.axis_size("cols")
    rows = columns // BLOCK_COLS
    surf_cells = sea_state.shape[1]
    surf_rows = surf_cells // LANES
    capacity = slot_cell.shape[0] // (2 * ring)
    cap_rows = max(4, -(-capacity // LANES))

    parts, ratios, below, sea = forward(
        jnp.swapaxes(air_state, 0, 1),
        mix_coef,
        flux_scale.reshape(rows, LANES),
        sea_state,
        sea_rate.reshape(surf_rows, LANES),
        block_counts,
        cell_column.reshape(-1, LANES),
        cell_owner.reshape(-1, LANES),
        cell_coef.reshape(-1, LANES),
        cell_weight.reshape(-1, LANES),
        slot_cell.reshape(-1, LANES),
        slot_frac.reshape(-1, LANES),
        ring,
        cap_rows,
        capacity,
    )
    air_new, sea_new = ascend(parts, ratios, below, sea.reshape(tracers, surf_rows, LANES))
    return jnp.swapaxes(air_new, 0, 1), sea_new


def solution(mesh):
    return jax.shard_map(
        body,
        mesh=mesh,
        in_specs=(
            P("sect", None, "cols"),
            P("sect", "cols"),
            P("cols"),
            P(None, ("sect", "cols")),
            P(("sect", "cols")),
            P(("sect", "cols"), None),
            P(("sect", "cols")),
            P(("sect", "cols"), None),
            P(("sect", "cols")),
            P(("sect", "cols")),
            P(("sect", "cols")),
            P(("sect", "cols")),
        ),
        out_specs=(P("sect", None, "cols"), P(None, ("sect", "cols"))),
        check_vma=False,
    )
```
